128 devices in a mesh: wide: 16 (over x_lo, z, core), narrow: 8 (over y, x_hi).
Axes of the slice: x: 4 (x_hi: 2, x_lo: 2; x = x_hi * 2 + x_lo), y: 4, z: 4, core: 2. Of those that a mesh axis runs over, the one named last changes fastest.
Arguments:
- cotangent: bfloat16 [16, 128, 128, 128], P('wide', 'narrow'), may hold values from -6 to 6
- decoder_kernel: bfloat16 [512, 9, 16], replicated, may hold values from -0.09375 to 0.09375
- patch_projection_rows: bfloat16 [64, 3072], replicated, may hold values from -1.3 to 1.3
- stored_hidden_state: bfloat16 [4, 4096, 3072], P(None, 'wide'), may hold values from -160 to 160
- output_norm_scale: bfloat16 [4, 3072], replicated, may hold values from -2.5 to 2.5
- output_gate: bfloat16 [4, 3072], replicated, may hold values from -4 to 4
- preactivation_input: bfloat16 [4, 4096, 12288], P(None, 'wide', 'narrow'), may hold values from -6 to 6
- frozen_down_weight: bfloat16 [12288, 3072], P('narrow'), may hold values from -0.0546875 to 0.0546875
- adapter_down_rows: bfloat16 [12288, 64], P('narrow'), may hold values from -0.0546875 to 0.0546875
- adapter_up_rows: bfloat16 [64, 3072], replicated, may hold values from -0.75 to 0.75
Outputs:
- pre_grad: bfloat16 [4, 4096, 12288], P(None, 'wide', 'narrow')
- up_grad: float32 [3072, 64], P('wide')
- down_grad: float32 [12288, 64], P(('narrow', 'wide'))
The draws below stay inside these ranges and needn't reach their ends.
All inputs are finite; a program needn't handle non-finite values.
Results may differ from the reference program's by a relative error of at most 0.0065.
Values sent between devices are 32-bit elements; how exact they have to be, the bound alone decides.
A program may use at most 128 MiB of HBM per device.

```python
import math
import jax
import jax.numpy as jnp
from jax import lax

MODEL_WIDTH = 3072
MLP_UNITS = 12288
LAT_CH = 16
FEAT_CH = 512
ADAPTER_RANK = 64
GROUP = 4
LAT = 128
IMAGES = 4
SEQ = 4096
PATCH_FEAT = 64


def channel_profile(key):
    return jnp.clip(jax.random.normal(key, (MODEL_WIDTH,), jnp.float32), -4.0, 4.0)


def draw_patch_projection_rows(key, part):
    profile = channel_profile(key)
    key = jax.random.fold_in(key, 11)
    first, second = jax.random.split(key)
    loading = jnp.clip(jax.random.normal(first, (PATCH_FEAT, 1), jnp.float32), -3.0, 3.0)
    noise = jnp.clip(jax.random.normal(second, (PATCH_FEAT, MODEL_WIDTH), jnp.float32), -4.0, 4.0)
    value = (0.6 * loading * profile[None, :] + 0.8 * noise) * (1.0 / math.sqrt(PATCH_FEAT))
    return value.astype(jnp.bfloat16)


def draw_stored_hidden_state(key, part):
    profile = channel_profile(key)
    key = jax.random.fold_in(key, 23)
    first, second, third = jax.random.split(key, 3)
    row_scale = jnp.exp(jax.random.uniform(third, (IMAGES, SEQ, 1), jnp.float32, 0.0, math.log(10.0)))
    along = jnp.clip(jax.random.normal(first, (IMAGES, SEQ, 1), jnp.float32), -3.0, 3.0)
    noise = jnp.clip(jax.random.normal(second, (IMAGES, SEQ, MODEL_WIDTH), jnp.float32), -4.0, 4.0)
    value = row_scale * (along * profile[None, None, :] + noise)
    return value.astype(jnp.bfloat16)


def steps_of(own_key, shape, pieces, least, high):
    level, own = 1.0, jax.random.fold_in(own_key, 6)
    for axis_at, parts in pieces:
        heights = jnp.exp(jax.random.uniform(jax.random.fold_in(own, axis_at), (parts,), jnp.float32, least / len(pieces), high / len(pieces)))
        level = level * jnp.repeat(heights, shape[axis_at] // parts).reshape([-1 if axis == axis_at else 1 for axis in range(len(shape))])
    return level


def scatter_about(own_key, extent, spread, bound, shards=(), held_as=jnp.bfloat16):
    result = spread * jax.random.normal(own_key, extent, jnp.float32)
    if shards:
        result = result * steps_of(own_key, extent, shards, -0.22, 0.18)
    return jnp.clip(result, -bound, bound).astype(held_as)


def setup_inputs(seed: int = 0) -> dict:
    key_list = jax.random.split(jax.random.key(seed), 11)
    return {
        "cotangent": scatter_about(key_list[0], (IMAGES * GROUP, FEAT_CH // GROUP, LAT, LAT), 1.0, 6.0, ((0, 16), (1, 8))),
        "decoder_kernel": scatter_about(key_list[1], (FEAT_CH, 9, LAT_CH), (FEAT_CH * 9) ** -0.5, 0.09375),
        "patch_projection_rows": draw_patch_projection_rows(jax.random.fold_in(key_list[10], 71), 0),
        "stored_hidden_state": draw_stored_hidden_state(jax.random.fold_in(key_list[10], 71), 0),
        "output_norm_scale": scatter_about(key_list[4], (IMAGES, MODEL_WIDTH), 0.5, 2.5),
        "output_gate": scatter_about(key_list[5], (IMAGES, MODEL_WIDTH), 1.0, 4.0),
        "preactivation_input": scatter_about(key_list[6], (IMAGES, SEQ, MLP_UNITS), 1.0, 6.0, ((1, 16), (2, 8))),
        "frozen_down_weight": scatter_about(key_list[7], (MLP_UNITS, MODEL_WIDTH), MLP_UNITS ** -0.5, 0.0546875, ((0, 8),)),
        "adapter_down_rows": scatter_about(key_list[8], (MLP_UNITS, ADAPTER_RANK), MLP_UNITS ** -0.5, 0.0546875, ((0, 8),)),
        "adapter_up_rows": scatter_about(key_list[9], (ADAPTER_RANK, MODEL_WIDTH), ADAPTER_RANK ** -0.5, 0.75),
    }


vae_inverse = 1.0 / 0.3611

def gelu_parts(pre):
    m = pre.astype(jnp.float32)
    inner = 0.7978845608 * (m + 0.044715 * m * m * m)
    tval = jnp.tanh(inner)
    value = 0.5 * m * (1.0 + tval)
    slope = 0.5 * (1.0 + tval) + 0.5 * m * (1.0 - tval * tval) * 0.7978845608 * (1.0 + 0.134145 * m * m)
    return (value, slope)

def reference(cotangent, decoder_kernel, patch_projection_rows, stored_hidden_state, output_norm_scale, output_gate, preactivation_input, frozen_down_weight, adapter_down_rows, adapter_up_rows):
    features = cotangent.reshape(IMAGES, FEAT_CH, LAT, LAT)
    padded = jnp.pad(features, ((0, 0), (0, 0), (1, 1), (1, 1)))
    latent = jnp.zeros((IMAGES, LAT_CH, LAT, LAT), jnp.float32)
    for tap in range(9):
        row_tap = tap // 3
        col_tap = tap % 3
        piece = padded[:, :, 2 - row_tap:2 - row_tap + LAT, 2 - col_tap:2 - col_tap + LAT]
        latent = latent + jnp.einsum('co,bcyx->boyx', decoder_kernel[:, tap, :].astype(jnp.float32), piece.astype(jnp.float32))
    latent = latent * vae_inverse
    half = LAT // 2
    patches = latent.reshape(IMAGES, LAT_CH, half, 2, half, 2).transpose(0, 2, 4, 1, 3, 5).reshape(IMAGES, SEQ, PATCH_FEAT)
    patches = patches.astype(jnp.bfloat16)
    head_grad = jnp.einsum('bsp,pd->bsd', patches.astype(jnp.float32), patch_projection_rows.astype(jnp.float32))
    scaled = head_grad * (1.0 + output_norm_scale.astype(jnp.float32))[:, None, :]
    stored = stored_hidden_state.astype(jnp.float32)
    centered = stored - lax.optimization_barrier(jnp.mean(stored, axis=2, keepdims=True))
    inv_std = 1.0 / jnp.sqrt(lax.optimization_barrier(jnp.mean(centered * centered, axis=2, keepdims=True)) + 1e-06)
    normed = centered * inv_std
    inner_term = scaled - lax.optimization_barrier(jnp.mean(scaled, axis=2, keepdims=True)) - normed * lax.optimization_barrier(jnp.mean(scaled * normed, axis=2, keepdims=True))
    output_gradient = (output_gate.astype(jnp.float32)[:, None, :] * inv_std * inner_term).astype(jnp.bfloat16)
    value, slope = gelu_parts(preactivation_input)
    hidden_state = value.astype(jnp.bfloat16)
    norm = 1.0 / jnp.sqrt(jnp.float32(IMAGES * SEQ))
    reduced_value = (norm * jnp.einsum('hiy,yk->hik', hidden_state.astype(jnp.float32), adapter_down_rows.astype(jnp.float32))).astype(jnp.bfloat16)
    backward_pass = jnp.einsum('yqi,pi->yqp', output_gradient.astype(jnp.float32), adapter_up_rows.astype(jnp.float32)).astype(jnp.bfloat16)
    up_grad = jnp.einsum('bsd,bsr->dr', output_gradient.astype(jnp.float32), reduced_value.astype(jnp.float32))
    down_grad = norm * jnp.einsum('bsf,bsr->fr', hidden_state.astype(jnp.float32), backward_pass.astype(jnp.float32))
    hidden_state_gradient = jnp.einsum('bsd,fd->bsf', output_gradient.astype(jnp.float32), frozen_down_weight.astype(jnp.float32))
    hidden_state_gradient = hidden_state_gradient + jnp.einsum('pzu,lu->pzl', backward_pass.astype(jnp.float32), adapter_down_rows.astype(jnp.float32))
    pre_grad = (hidden_state_gradient * slope).astype(jnp.bfloat16)
    return (pre_grad, up_grad, down_grad)
```

```python
import functools

import jax
import jax.numpy as jnp
import numpy as np
from jax import lax
from jax.experimental import pallas as pl
from jax.experimental.pallas import tpu as pltpu
from jax.sharding import PartitionSpec as P

MESH = pl.DeviceIdType.MESH
F32 = jnp.float32
BF16 = jnp.bfloat16
D = 3072
F = 1536
VAE_INVERSE = 1.0 / 0.3611
NORM = 1.0 / 128.0
GELU_A = 0.7978845608
MIB = 1 << 20


def dot_nt(a, b):
    return lax.dot_general(a, b, (((1,), (1,)), ((), ())), preferred_element_type=F32)


def dot_nn(a, b):
    return lax.dot_general(a, b, (((1,), (0,)), ((), ())), preferred_element_type=F32)


def dot_tn(a, b):
    return lax.dot_general(a, b, (((0,), (0,)), ((), ())), preferred_element_type=F32)


def column_taps():
    out = np.zeros((128, 512), np.float32)
    for tap in range(4):
        for q in range(64):
            col = 2 * q - 1 + tap
            if 0 <= col < 128:
                out[col, 128 * tap + q] = 1
                out[col, 128 * tap + 64 + q] = 1
    return out


def kernel_taps():
    out = np.zeros((144, 1024), np.float32)
    for ty in range(4):
        for tx in range(4):
            for i in range(2):
                for j in range(2):
                    dy, dx = i + 2 - ty, j + 2 - tx
                    if 0 <= dy < 3 and 0 <= dx < 3:
                        for o in range(16):
                            out[(3 * dy + dx) * 16 + o, (4 * ty + tx) * 64 + 4 * o + 2 * i + j] = 1
    return out


def conv_kernel(ft_ref, k_ref, s_ref, sel_ref, out_ref, g_ref, w_ref):
    zero = jnp.zeros((16, 128), BF16)
    for tap in range(4):
        g_ref[tap, 0] = zero
        g_ref[tap, 129] = zero

    @pl.loop(0, 8)
    def _(block):
        rows = ft_ref[pl.ds(pl.multiple_of(block * 256, 256), 256), :]
        for tap in range(4):
            moved = dot_nn(rows, s_ref[:, 128 * tap : 128 * tap + 128])
            g_ref[tap, pl.ds(1 + block * 16, 16)] = moved.astype(BF16).reshape(16, 16, 128)

    taps = dot_nn(k_ref[...], sel_ref[...]).astype(BF16)
    for t in range(16):
        w_ref[16 * t : 16 * t + 16, :] = taps[:, 64 * t : 64 * t + 64]
    weights = w_ref[...]
    left = lax.broadcasted_iota(jnp.int32, (16, 128), 1) < 64

    @pl.loop(0, 4)
    def _(quarter):
        for z in range(2):
            for c in range(2):
                for half in range(2):
                    row = 32 * quarter + 16 * z + 8 * c + 4 * half
                    window = [
                        jnp.where(left, g_ref[tx, row + ty], g_ref[tx, row + 2 + ty])
                        for ty in range(4)
                        for tx in range(4)
                    ]
                    out_ref[c, 8 * z + 2 * quarter + half] = dot_tn(weights, jnp.concatenate(window, 0))


def conv(cotangent, kernel):
    ft = cotangent[0].transpose(1, 0, 2).reshape(2048, 128)
    return pl.pallas_call(
        conv_kernel,
        out_shape=jax.ShapeDtypeStruct((2, 16, 64, 128), F32),
        scratch_shapes=[pltpu.VMEM((4, 130, 16, 128), BF16), pltpu.VMEM((256, 64), BF16)],
        compiler_params=pltpu.CompilerParams(vmem_limit_bytes=16 * MIB),
        name="conv",
    )(ft, kernel, jnp.asarray(column_taps(), BF16), jnp.asarray(kernel_taps(), BF16))


def main_kernel(
    part,
    stored,
    pre,
    weight,
    a_ref,
    u_ref,
    p_ref,
    scale_ref,
    gate_ref,
    pre_out,
    up_out,
    down_out,
    own,
    recv_a,
    recv_b,
    red,
    recv_c,
    low_part,
    recv_l,
    red_l,
    recv_m,
    ubuf,
    recv_u,
    red_u,
    recv_e,
    dbuf,
    recv_d,
    stored_v,
    pre_v,
    weight_v,
    zp,
    xw,
    hid,
    slope,
    nz,
    meanb,
    invb,
    vbt,
    ikcol,
    ltile,
    backt,
    klt,
    at_ref,
    gate_v,
    scale_v,
    sem_local,
    sem_pre,
    sem_stored,
    sem_weight,
    sem_out,
    send_a,
    got_a,
    send_b,
    got_b,
    send_c,
    got_c,
    send_l,
    got_l,
    send_m,
    got_m,
    send_u,
    got_u,
    send_e,
    got_e,
    send_d,
    got_d,
):
    w = lax.axis_index("wide")
    n = lax.axis_index("narrow")
    img = lax.div(w, 4)
    grp = lax.rem(w, 4)
    core = lax.rem(w, 2)
    me_b = lax.div(grp, 2) * 8 + n
    c_wide = 4 * lax.div(n, 2) + grp
    e_wide = 2 * n + lax.div(w, 8)
    c_self = c_wide == w
    e_self = e_wide == w

    own_copy = pltpu.make_async_copy(part.at[core], own, sem_local.at[0])
    own_copy.start()

    def pre_copy(i):
        return pltpu.make_async_copy(pre.at[i], pre_v.at[i], sem_pre.at[i])

    def stored_copy(i):
        return pltpu.make_async_copy(stored.at[i], stored_v.at[i], sem_stored.at[i])

    def weight_copy(j):
        rows = pl.ds(pl.multiple_of(j * 256, 256), 256)
        return pltpu.make_async_copy(weight.at[rows], weight_v.at[rows], sem_weight.at[j])

    def out_copy(i):
        return pltpu.make_async_copy(pre_v.at[i], pre_out.at[i], sem_out.at[i])

    @pl.loop(0, 4)
    def _(i):
        pre_copy(i).start()

    @pl.loop(0, 4)
    def _(i):
        stored_copy(i).start()

    @pl.loop(0, 6)
    def _(j):
        weight_copy(j).start()

    barrier = pltpu.get_barrier_semaphore()

    def greet(dw, dn):
        pl.semaphore_signal(barrier, inc=1, device_id=(dw, dn), device_id_type=MESH)

    def b_device(t):
        return 4 * img + 2 * lax.div(t, 8) + core, lax.rem(t, 8)

    @pl.loop(1, 16)
    def _(k):
        greet(*b_device(lax.rem(me_b + k, 16)))
        greet(lax.rem(w + k, 16), n)

    @pl.loop(0, 8)
    def _(k):
        cw, cn = 4 * lax.div(k, 2) + grp, 2 * img + lax.rem(k, 2)

        @pl.when(jnp.logical_or(cw != w, cn != n))
        def _():
            greet(cw, cn)

        ew, en = 8 * core + k, lax.div(w, 2)

        @pl.when(jnp.logical_or(ew != w, en != n))
        def _():
            greet(ew, en)

    pl.semaphore_wait(barrier, 46 - c_self.astype(jnp.int32) - e_self.astype(jnp.int32))

    copy_a = pltpu.make_async_remote_copy(
        src_ref=part.at[1 - core],
        dst_ref=recv_a,
        send_sem=send_a.at[0],
        recv_sem=got_a.at[0],
        device_id=(w + 1 - 2 * core, n),
        device_id_type=MESH,
    )
    copy_a.start()

    eye = (
        lax.broadcasted_iota(jnp.int32, (64, 64), 0) == lax.broadcasted_iota(jnp.int32, (64, 64), 1)
    ).astype(F32).astype(BF16)
    at_ref[...] = dot_nt(eye, a_ref[...]).astype(BF16)

    def copy_b(src, slot, t, dev):
        return pltpu.make_async_remote_copy(
            src_ref=own.at[src],
            dst_ref=recv_b.at[slot],
            send_sem=send_b.at[t],
            recv_sem=got_b.at[slot],
            device_id=dev,
            device_id_type=MESH,
        )

    def start_b():
        own_copy.wait()
        copy_a.wait()

        @pl.loop(1, 17)
        def _(k):
            t = lax.rem(me_b + k, 16)
            own[t] = own[t] + recv_a[t]

            @pl.when(k < 16)
            def _():
                copy_b(t, me_b, t, b_device(t)).start()

    gates = gate_ref[...].astype(F32)
    scales = 1.0 + scale_ref[...].astype(F32)
    for i in range(4):
        gate_v[i] = jnp.broadcast_to(gates[i : i + 1], (8, D))
        scale_v[i] = jnp.broadcast_to(scales[i : i + 1], (8, D))

    @pl.loop(0, 4)
    def _(i):
        pre_copy(i).wait()

        @pl.loop(0, 16)
        def _(r):
            rows = pl.ds(pl.multiple_of(r * 16, 16), 16)
            here = pl.ds(pl.multiple_of(i * 256 + r * 16, 16), 16)
            for s in range(3):
                cols = slice(512 * s, 512 * s + 512)
                m = pre_v[i, rows, cols].astype(F32)
                sq = m * m
                h = 0.5 + 0.5 * jnp.tanh(m * (GELU_A + (GELU_A * 0.044715) * sq))
                val = m * h
                hid[here, cols] = val.astype(BF16)
                slope[here, cols] = h + (2.0 * val) * (1.0 - h) * (
                    GELU_A + (GELU_A * 0.134145) * sq
                )

        rows = pl.ds(pl.multiple_of(i * 256, 256), 256)
        lt = dot_nt(at_ref[...], hid[rows, :])
        low_part[2 * i] = lt[:, :128]
        low_part[2 * i + 1] = lt[:, 128:]

        @pl.when(i == 0)
        def _():
            start_b()

    def copy_l(t, slot):
        return pltpu.make_async_remote_copy(
            src_ref=low_part.at[t],
            dst_ref=recv_l.at[slot],
            send_sem=send_l.at[t],
            recv_sem=got_l.at[slot],
            device_id=(w, t),
            device_id_type=MESH,
        )

    @pl.loop(1, 8)
    def _(k):
        copy_l(lax.rem(n + k, 8), n).start()

    @pl.loop(0, 4)
    def _(i):
        stored_copy(i).wait()
        gate = gate_v[i, 0:1, :]
        scale = scale_v[i, 0:1, :]

        @pl.loop(0, 16)
        def _(r):
            rows = pl.ds(pl.multiple_of(r * 16, 16), 16)
            here = pl.ds(pl.multiple_of(i * 256 + r * 16, 16), 16)
            x = stored_v[i, rows, :].astype(F32)
            mean = jnp.sum(x, axis=1, keepdims=True) * (1.0 / D)
            x = x - mean
            var = jnp.sum(x * x, axis=1, keepdims=True) * (1.0 / D)
            zp[here, :] = (x * gate).astype(BF16)
            meanb[here, :] = jnp.broadcast_to(mean, (16, 128))
            invb[here, :] = jnp.broadcast_to(1.0 / jnp.sqrt(var + 1e-06), (16, 128))

        @pl.loop(0, 4)
        def _(r):
            rows = pl.ds(pl.multiple_of(r * 16, 16), 16)
            rows2 = pl.ds(pl.multiple_of(64 + r * 16, 16), 16)
            here = pl.ds(pl.multiple_of(1024 + 64 * i + r * 16, 16), 16)
            x = p_ref[rows, :].astype(F32) * scale
            x = x - jnp.sum(x, axis=1, keepdims=True) * (1.0 / D)
            xw[rows, :] = x.astype(BF16)
            zp[here, :] = (x * gate).astype(BF16)
            xw[rows2, :] = (u_ref[rows, :].astype(F32) * gate).astype(BF16)

        tokens = pl.ds(pl.multiple_of(i * 256, 256), 256)
        xs = xw[...]
        mean_row = jnp.transpose(meanb[tokens, :])[:1, :]
        sums = jnp.sum(xs.astype(F32), axis=1, keepdims=True)
        vbt[i] = dot_nt(xs, stored_v[i]) - sums * mean_row

    def copy_c(dn, slot):
        return pltpu.make_async_remote_copy(
            src_ref=red,
            dst_ref=recv_c.at[slot],
            send_sem=send_c.at[dn],
            recv_sem=got_c.at[slot],
            device_id=(c_wide, dn),
            device_id_type=MESH,
        )

    my_c_slot = 2 * img + lax.rem(n, 2)
    total = own[me_b]
    red[...] = total

    @pl.loop(1, 16)
    def _(k):
        t = lax.rem(me_b + k, 16)
        copy_b(t, t, t, b_device(t)).wait_recv()
        red[...] += recv_b[t]

    @pl.loop(1, 9)
    def _(k):
        dn = lax.rem(n + k, 8)

        @pl.when(jnp.logical_or(k < 8, jnp.logical_not(c_self)))
        def _():
            copy_c(dn, my_c_slot).start()

    @pl.when(c_self)
    def _():
        recv_c[my_c_slot] = red[...]

    def copy_m(t, slot):
        return pltpu.make_async_remote_copy(
            src_ref=red_l,
            dst_ref=recv_m.at[slot],
            send_sem=send_m.at[t],
            recv_sem=got_m.at[slot],
            device_id=(w, t),
            device_id_type=MESH,
        )

    red_l[...] = low_part[n]

    @pl.loop(1, 8)
    def _(k):
        t = lax.rem(n + k, 8)
        copy_l(t, t).wait_recv()
        red_l[...] += recv_l[t]

    recv_m[n] = red_l[...]

    @pl.loop(1, 8)
    def _(k):
        copy_m(lax.rem(n + k, 8), n).start()

    @pl.loop(0, 6)
    def _(j):
        weight_copy(j).wait()
        rows = pl.ds(pl.multiple_of(j * 256, 256), 256)
        nz[j] = dot_nt(zp[...], weight_v[rows, :])

    put = dot_nt(u_ref[...], zp[1024:1280, :])

    @pl.loop(0, 8)
    def _(k):
        sw, sn = 4 * lax.div(k, 2) + grp, 2 * img + lax.rem(k, 2)

        @pl.when(jnp.logical_or(sw != w, sn != n))
        def _():
            copy_c(0, k).wait_recv()

    @pl.loop(1, 8)
    def _(k):
        t = lax.rem(n + k, 8)
        copy_m(t, t).wait_recv()

    t1 = []
    for i in range(4):
        tok = slice(256 * i, 256 * i + 256)
        lat = jnp.concatenate([recv_c[2 * i], recv_c[2 * i + 1]], 1)
        pat = (lat * VAE_INVERSE).astype(BF16)
        pf = pat.astype(F32)
        inv = jnp.transpose(invb[tok, :])[:1, :]
        vb = vbt[i]
        k_row = inv * inv * (jnp.sum(pf * vb[:64], axis=0, keepdims=True) * (1.0 / D))
        pu = put[:, 64 * i : 64 * i + 64]
        pu_hi = pu.astype(BF16)
        pu_lo = (pu - pu_hi.astype(F32)).astype(BF16)
        back = (inv * (dot_nn(pu_hi, pat) + dot_nn(pu_lo, pat) - k_row * vb[64:])).astype(BF16)
        ip = inv * pf
        ip_hi = ip.astype(BF16)
        ip_lo = (ip - ip_hi.astype(F32)).astype(BF16)
        backt[:, tok] = back
        stack = jnp.concatenate([ip_hi, ip_lo, ip_hi, back], 0)
        ltile[tok, :] = jnp.transpose(stack.astype(F32)).astype(BF16)
        ik = inv * k_row
        ikcol[tok, :] = jnp.transpose(jnp.broadcast_to(ik, (128, 256)))
        low = (jnp.concatenate([recv_m[2 * i], recv_m[2 * i + 1]], 1) * NORM).astype(BF16)
        klt[:, tok] = (-ik * low.astype(F32)).astype(BF16)
        t1.append(dot_nt(low, ip_hi) + dot_nt(low, ip_lo))
    klt[:, 1024:1280] = jnp.concatenate(t1, 1).astype(BF16)

    up_t = dot_nn(klt[...], zp[:, pl.ds(pl.multiple_of(n * 384, 128), 384)])
    ubuf[0] = up_t[:, :256]
    ubuf[1] = pltpu.roll(up_t[:, 128:384], 192, 1)

    def copy_u(t, slot):
        return pltpu.make_async_remote_copy(
            src_ref=ubuf.at[lax.div(t, 8), pl.ds(pl.multiple_of(lax.rem(t, 8) * 8, 8), 8)],
            dst_ref=recv_u.at[slot],
            send_sem=send_u.at[t],
            recv_sem=got_u.at[slot],
            device_id=(t, n),
            device_id_type=MESH,
        )

    @pl.loop(1, 16)
    def _(k):
        copy_u(lax.rem(w + k, 16), w).start()

    down_t = dot_nn(backt[...], hid[...]) * NORM
    for t in range(16):
        first = 96 * t // 128 * 128
        off = 96 * t - first
        if off + 96 <= 128:
            piece = down_t[:, first : first + 128]
            piece = pltpu.roll(piece, 128 - off, 1) if off else piece
        else:
            piece = pltpu.roll(down_t[:, first : first + 256], 256 - off, 1)[:, :128]
        dbuf[t] = piece

    def copy_d(t, slot):
        return pltpu.make_async_remote_copy(
            src_ref=dbuf.at[t],
            dst_ref=recv_d.at[slot],
            send_sem=send_d.at[t],
            recv_sem=got_d.at[slot],
            device_id=(t, n),
            device_id_type=MESH,
        )

    @pl.loop(1, 16)
    def _(k):
        copy_d(lax.rem(w + k, 16), w).start()

    @pl.loop(0, 4)
    def _(i):
        rows = pl.ds(pl.multiple_of(i * 256, 256), 256)
        left = ltile[rows, :]
        coef = ikcol[rows, :]
        coef = jnp.concatenate([coef, coef], 1)
        for j in range(6):
            cols = slice(256 * j, 256 * j + 256)
            q = nz[j, pl.ds(pl.multiple_of(1024 + 64 * i, 64), 64), :]
            q_hi = q.astype(BF16)
            q_lo = (q - q_hi.astype(F32)).astype(BF16)
            right = jnp.concatenate([q_hi, q_hi, q_lo, at_ref[:, cols]], 0)
            grad = dot_nn(left, right) - coef * nz[j, rows, :]
            pre_v[i, :, cols] = (grad * slope[rows, cols]).astype(BF16)
        out_copy(i).start()

    def copy_e(dn, slot):
        return pltpu.make_async_remote_copy(
            src_ref=red_u,
            dst_ref=recv_e.at[slot],
            send_sem=send_e.at[dn],
            recv_sem=got_e.at[slot],
            device_id=(e_wide, dn),
            device_id_type=MESH,
        )

    my_e_slot = lax.rem(w, 8)
    red_u[...] = ubuf[lax.div(w, 8), pl.ds(pl.multiple_of(my_e_slot * 8, 8), 8)]

    @pl.loop(1, 16)
    def _(k):
        t = lax.rem(w + k, 16)
        copy_u(t, t).wait_recv()
        red_u[...] += recv_u[t]

    @pl.loop(1, 9)
    def _(k):
        dn = lax.rem(n + k, 8)

        @pl.when(jnp.logical_or(k < 8, jnp.logical_not(e_self)))
        def _():
            copy_e(dn, my_e_slot).start()

    @pl.when(e_self)
    def _():
        recv_e[my_e_slot] = red_u[...]

    recv_d[w] = dbuf[w]

    @pl.loop(1, 16)
    def _(k):
        t = lax.rem(w + k, 16)
        copy_d(t, t).wait_recv()

    down = recv_d[0]
    for t in range(1, 16):
        down = down + recv_d[t]
    down_out[...] = jnp.transpose(down)[:96, :]

    @pl.loop(0, 8)
    def _(k):
        @pl.when(jnp.logical_or(8 * core + k != w, lax.div(w, 2) != n))
        def _():
            copy_e(0, k).wait_recv()

    up = jnp.concatenate([recv_e[k] for k in range(8)], 0)
    up_out[...] = jnp.transpose(up)[:192, :]

    @pl.loop(1, 16)
    def _(k):
        t = lax.rem(me_b + k, 16)
        copy_b(t, t, t, b_device(t)).wait_send()
        t = lax.rem(w + k, 16)
        copy_u(t, t).wait_send()
        copy_d(t, t).wait_send()

    @pl.loop(1, 9)
    def _(k):
        dn = lax.rem(n + k, 8)

        @pl.when(k < 8)
        def _():
            copy_l(dn, n).wait_send()
            copy_m(dn, n).wait_send()

        @pl.when(jnp.logical_or(k < 8, jnp.logical_not(c_self)))
        def _():
            copy_c(dn, my_c_slot).wait_send()

        @pl.when(jnp.logical_or(k < 8, jnp.logical_not(e_self)))
        def _():
            copy_e(dn, my_e_slot).wait_send()

    @pl.loop(0, 4)
    def _(i):
        out_copy(i).wait()


def main(part, stored, pre, weight, a, u, p, scale, gate):
    dma = pltpu.SemaphoreType.DMA
    v = pltpu.VMEM
    anywhere = pl.BlockSpec(memory_space=pl.ANY)
    vmem = pl.BlockSpec(memory_space=pltpu.VMEM)
    return pl.pallas_call(
        main_kernel,
        out_shape=(
            jax.ShapeDtypeStruct((4, 256, F), BF16),
            jax.ShapeDtypeStruct((192, 64), F32),
            jax.ShapeDtypeStruct((96, 64), F32),
        ),
        in_specs=[anywhere] * 4 + [vmem] * 5,
        out_specs=(anywhere, vmem, vmem),
        scratch_shapes=[
            v((16, 64, 128), F32),
            v((16, 64, 128), F32),
            v((16, 64, 128), F32),
            v((64, 128), F32),
            v((8, 64, 128), F32),
            v((8, 64, 128), F32),
            v((8, 64, 128), F32),
            v((64, 128), F32),
            v((8, 64, 128), F32),
            v((2, 64, 256), F32),
            v((16, 8, 256), F32),
            v((8, 256), F32),
            v((8, 8, 256), F32),
            v((16, 64, 128), F32),
            v((16, 64, 128), F32),
            v((4, 256, D), BF16),
            v((4, 256, F), BF16),
            v((F, D), BF16),
            v((1280, D), BF16),
            v((128, D), BF16),
            v((1024, F), BF16),
            v((1024, F), F32),
            v((6, 1280, 256), F32),
            v((1024, 128), F32),
            v((1024, 128), F32),
            v((4, 128, 256), F32),
            v((1024, 128), F32),
            v((1024, 256), BF16),
            v((64, 1024), BF16),
            v((64, 1280), BF16),
            v((64, F), BF16),
            v((4, 8, D), F32),
            v((4, 8, D), F32),
            dma((1,)),
            dma((4,)),
            dma((4,)),
            dma((6,)),
            dma((4,)),
            dma((1,)),
            dma((1,)),
            dma((16,)),
            dma((16,)),
            dma((8,)),
            dma((8,)),
            dma((8,)),
            dma((8,)),
            dma((8,)),
            dma((8,)),
            dma((16,)),
            dma((16,)),
            dma((8,)),
            dma((8,)),
            dma((16,)),
            dma((16,)),
        ],
        compiler_params=pltpu.CompilerParams(
            collective_id=0, has_side_effects=True, vmem_limit_bytes=60 * MIB
        ),
        name="main",
    )(part, stored, pre, weight, a, u, p, scale, gate)


def local(
    cotangent,
    decoder_kernel,
    patch_projection_rows,
    stored_hidden_state,
    output_norm_scale,
    output_gate,
    preactivation_input,
    frozen_down_weight,
    adapter_down_rows,
    adapter_up_rows,
):
    offset = lax.axis_index("wide") % 4 * 128 + lax.axis_index("narrow") * 16
    kernel = lax.dynamic_slice_in_dim(decoder_kernel, offset, 16, 0).reshape(16, 144)
    part = conv(cotangent, kernel)
    return main(
        part,
        stored_hidden_state,
        preactivation_input,
        frozen_down_weight,
        adapter_down_rows,
        adapter_up_rows,
        patch_projection_rows,
        output_norm_scale,
        output_gate,
    )


def solution(mesh):
    placed = (
        P("wide", "narrow", None, None),
        P(),
        P(),
        P(None, "wide", None),
        P(),
        P(),
        P(None, "wide", "narrow"),
        P("narrow", None),
        P("narrow", None),
        P(),
    )
    return jax.shard_map(
        local,
        mesh=mesh,
        in_specs=placed,
        out_specs=(P(None, "wide", "narrow"), P("wide", None), P(("narrow", "wide"), None)),
        check_vma=False,
    )
```

```python
import jax
import jax.numpy as jnp
from jax import lax
from jax.experimental import pallas as pl
from jax.experimental.pallas import tpu as pltpu
from jax.sharding import PartitionSpec as P

MESH = pl.DeviceIdType.MESH
F32 = jnp.float32
BF16 = jnp.bfloat16
D = 3072
F = 1536
VAE_INVERSE = 1.0 / 0.3611
NORM = 1.0 / 128.0
GELU_A = 0.7978845608
MIB = 1 << 20


def dot_nt(a, b):
    return lax.dot_general(a, b, (((1,), (1,)), ((), ())), preferred_element_type=F32)


def dot_nn(a, b):
    return lax.dot_general(a, b, (((1,), (0,)), ((), ())), preferred_element_type=F32)


def dot_tn(a, b):
    return lax.dot_general(a, b, (((0,), (0,)), ((), ())), preferred_element_type=F32)


def iota(shape, axis):
    return lax.broadcasted_iota(jnp.int32, shape, axis)


def one_hot(mask):
    return mask.astype(F32).astype(BF16)


def column_taps():
    col = iota((128, 512), 1)
    return one_hot(iota((128, 512), 0) == 2 * (col & 63) - 1 + (col >> 7))


def kernel_taps():
    col = iota((16, 1024), 1)
    same = iota((16, 1024), 0) == (col & 63) >> 2
    dy = ((col >> 1) & 1) + 2 - (col >> 8)
    dx = (col & 1) + 2 - ((col >> 6) & 3)
    return jnp.concatenate(
        [one_hot(same & (dy == t // 3) & (dx == t % 3)) for t in range(9)], 0
    )


def main_kernel(
    cot,
    taps_in,
    stored,
    pre,
    weight,
    a_in,
    u_in,
    p_in,
    scale_in,
    gate_in,
    pre_out,
    up_out,
    down_out,
    give,
    own,
    recv_a,
    recv_b,
    red,
    recv_c,
    low_part,
    recv_l,
    red_l,
    recv_m,
    ubuf,
    recv_u,
    red_u,
    recv_e,
    dbuf,
    recv_d,
    stored_v,
    pre_v,
    weight_v,
    zp,
    xw,
    hid,
    nz,
    prod,
    cot_v,
    taps_v,
    g_ref,
    u_ref,
    p_ref,
    scale_ref,
    gate_ref,
    meanb,
    invb,
    vbt,
    ikcol,
    ltile,
    backt,
    klt,
    at_ref,
    gate_v,
    scale_v,
    sem_local,
    sem_pre,
    sem_stored,
    sem_weight,
    sem_out,
    send_a,
    got_a,
    send_b,
    got_b,
    send_c,
    got_c,
    send_l,
    got_l,
    send_m,
    got_m,
    send_u,
    got_u,
    send_e,
    got_e,
    send_d,
    got_d,
):
    w = lax.axis_index("wide")
    n = lax.axis_index("narrow")
    img = lax.div(w, 4)
    grp = lax.rem(w, 4)
    core = lax.rem(w, 2)
    me_b = lax.div(grp, 2) * 8 + n
    c_wide = 4 * lax.div(n, 2) + grp
    e_wide = 2 * n + lax.div(w, 8)
    c_self = c_wide == w
    e_self = e_wide == w

    small = [
        pltpu.make_async_copy(src, dst, sem_local.at[k])
        for k, (src, dst) in enumerate(
            [
                (cot, cot_v),
                (taps_in, taps_v),
                (a_in, at_ref),
                (gate_in, gate_ref),
                (scale_in, scale_ref),
                (p_in, p_ref),
                (u_in, u_ref),
            ]
        )
    ]
    for copy in small:
        copy.start()

    def pre_copy(i):
        return pltpu.make_async_copy(pre.at[i], pre_v.at[i], sem_pre.at[i])

    def stored_copy(i):
        return pltpu.make_async_copy(stored.at[i], stored_v.at[i], sem_stored.at[i])

    def weight_copy(j):
        rows = pl.ds(pl.multiple_of(j * 256, 256), 256)
        return pltpu.make_async_copy(weight.at[rows], weight_v.at[rows], sem_weight.at[j])

    def out_copy(i):
        return pltpu.make_async_copy(pre_v.at[i], pre_out.at[i], sem_out.at[i])

    @pl.loop(0, 4)
    def _(i):
        pre_copy(i).start()

    @pl.loop(0, 4)
    def _(i):
        stored_copy(i).start()

    @pl.loop(0, 6)
    def _(j):
        weight_copy(j).start()

    barrier = pltpu.get_barrier_semaphore()

    def greet(dw, dn):
        pl.semaphore_signal(barrier, inc=1, device_id=(dw, dn), device_id_type=MESH)

    def b_device(t):
        return 4 * img + 2 * lax.div(t, 8) + core, lax.rem(t, 8)

    @pl.loop(1, 16)
    def _(k):
        greet(*b_device(lax.rem(me_b + k, 16)))
        greet(lax.rem(w + k, 16), n)

    @pl.loop(0, 8)
    def _(k):
        cw, cn = 4 * lax.div(k, 2) + grp, 2 * img + lax.rem(k, 2)

        @pl.when(jnp.logical_or(cw != w, cn != n))
        def _():
            greet(cw, cn)

        ew, en = 8 * core + k, lax.div(w, 2)

        @pl.when(jnp.logical_or(ew != w, en != n))
        def _():
            greet(ew, en)

    zero = jnp.zeros((16, 128), BF16)
    for tap in range(4):
        g_ref[tap, 0] = zero
        g_ref[tap, 129] = zero
    columns = column_taps()
    routes = kernel_taps()
    small[0].wait()

    @pl.loop(0, 4)
    def _(r):
        rows = cot_v[:, pl.ds(pl.multiple_of(r * 32, 32), 32), :]
        moved = dot_nn(jnp.swapaxes(rows, 0, 1).reshape(512, 128), columns)
        for tap in range(4):
            g_ref[tap, pl.ds(1 + r * 32, 32)] = (
                moved[:, 128 * tap : 128 * tap + 128].astype(BF16).reshape(32, 16, 128)
            )

    small[1].wait()
    pick = one_hot(iota((16, 512), 1) - grp * 128 - n * 16 == iota((16, 512), 0))
    mine = dot_nn(dot_nt(pick, taps_v[...]).astype(BF16), routes)
    mine = jnp.concatenate([mine[:, 64 * t : 64 * t + 64] for t in range(16)], 0)
    weights = jnp.transpose(mine).astype(BF16)
    left_half = iota((16, 128), 1) < 64

    def conv(side, dst):
        @pl.loop(0, 4)
        def _(quarter):
            for z in range(2):
                for half in range(2):
                    row = 32 * quarter + 16 * z + 8 * side + 4 * half
                    window = [
                        jnp.where(left_half, g_ref[tx, row + ty], g_ref[tx, row + 2 + ty])
                        for ty in range(4)
                        for tx in range(4)
                    ]
                    dst[8 * z + 2 * quarter + half] = dot_nn(
                        weights, jnp.concatenate(window, 0)
                    )

    conv(1 - core, give)
    pl.semaphore_wait(barrier, 46 - c_self.astype(jnp.int32) - e_self.astype(jnp.int32))

    copy_a = pltpu.make_async_remote_copy(
        src_ref=give,
        dst_ref=recv_a,
        send_sem=send_a.at[0],
        recv_sem=got_a.at[0],
        device_id=(w + 1 - 2 * core, n),
        device_id_type=MESH,
    )
    copy_a.start()
    conv(core, own)
    for copy in small[2:]:
        copy.wait()

    def copy_b(src, slot, t, dev):
        return pltpu.make_async_remote_copy(
            src_ref=own.at[src],
            dst_ref=recv_b.at[slot],
            send_sem=send_b.at[t],
            recv_sem=got_b.at[slot],
            device_id=dev,
            device_id_type=MESH,
        )

    def start_b():
        copy_a.wait()

        @pl.loop(1, 17)
        def _(k):
            t = lax.rem(me_b + k, 16)
            own[t] = own[t] + recv_a[t]

            @pl.when(k < 16)
            def _():
                copy_b(t, me_b, t, b_device(t)).start()

    gates = gate_ref[...].astype(F32)
    scales = 1.0 + scale_ref[...].astype(F32)
    for i in range(4):
        gate_v[i] = jnp.broadcast_to(gates[i : i + 1], (8, D))
        scale_v[i] = jnp.broadcast_to(scales[i : i + 1], (8, D))

    @pl.loop(0, 4)
    def _(i):
        pre_copy(i).wait()

        @pl.loop(0, 16)
        def _(r):
            rows = pl.ds(pl.multiple_of(r * 16, 16), 16)
            here = pl.ds(pl.multiple_of(i * 256 + r * 16, 16), 16)
            for s in range(3):
                cols = slice(512 * s, 512 * s + 512)
                m = pre_v[i, rows, cols].astype(F32)
                sq = m * m
                h = 0.5 + 0.5 * jnp.tanh(m * (GELU_A + (GELU_A * 0.044715) * sq))
                hid[here, cols] = (m * h).astype(BF16)

        rows = pl.ds(pl.multiple_of(i * 256, 256), 256)
        lt = dot_nt(at_ref[...], hid[rows, :])
        low_part[2 * i] = lt[:, :128]
        low_part[2 * i + 1] = lt[:, 128:]

        @pl.when(i == 0)
        def _():
            start_b()

    def copy_l(t, slot):
        return pltpu.make_async_remote_copy(
            src_ref=low_part.at[t],
            dst_ref=recv_l.at[slot],
            send_sem=send_l.at[t],
            recv_sem=got_l.at[slot],
            device_id=(w, t),
            device_id_type=MESH,
        )

    @pl.loop(1, 8)
    def _(k):
        copy_l(lax.rem(n + k, 8), n).start()

    @pl.loop(0, 4)
    def _(i):
        stored_copy(i).wait()

        @pl.loop(0, 16, unroll=4)
        def _(r):
            here = pl.ds(pl.multiple_of(i * 256 + r * 16, 16), 16)
            acc = jnp.zeros((16, 128), F32)
            for s in range(24):
                cols = slice(128 * s, 128 * s + 128)
                acc += stored_v[i, pl.ds(pl.multiple_of(r * 16, 16), 16), cols].astype(F32)
            meanb[here, :] = acc

        tokens = pl.ds(pl.multiple_of(i * 256, 256), 256)
        mean = jnp.sum(meanb[tokens, :], axis=1, keepdims=True) * (1.0 / D)
        meanb[tokens, :] = jnp.broadcast_to(mean, (256, 128))

        @pl.loop(0, 16, unroll=4)
        def _(r):
            here = pl.ds(pl.multiple_of(i * 256 + r * 16, 16), 16)
            mean = meanb[here, :]
            acc = jnp.zeros((16, 128), F32)
            for s in range(24):
                cols = slice(128 * s, 128 * s + 128)
                x = stored_v[i, pl.ds(pl.multiple_of(r * 16, 16), 16), cols].astype(F32) - mean
                zp[here, cols] = (x * gate_v[i, 0:1, cols]).astype(BF16)
                acc += x * x
            invb[here, :] = acc

        var = jnp.sum(invb[tokens, :], axis=1, keepdims=True) * (1.0 / D)
        invb[tokens, :] = jnp.broadcast_to(1.0 / jnp.sqrt(var + 1e-06), (256, 128))

        acc = jnp.zeros((64, 128), F32)
        for s in range(24):
            cols = slice(128 * s, 128 * s + 128)
            acc += p_ref[:, cols].astype(F32) * scale_v[i, 0:1, cols]
        mean = jnp.broadcast_to(jnp.sum(acc, axis=1, keepdims=True) * (1.0 / D), (64, 128))
        acc = jnp.zeros((128, 128), F32)
        here = pl.ds(pl.multiple_of(1024 + 64 * i, 64), 64)
        for s in range(24):
            cols = slice(128 * s, 128 * s + 128)
            gate = gate_v[i, 0:1, cols]
            x = p_ref[:, cols].astype(F32) * scale_v[i, 0:1, cols] - mean
            zp[here, cols] = (x * gate).astype(BF16)
            both = jnp.concatenate([x, u_ref[:, cols].astype(F32) * gate], 0).astype(BF16)
            xw[:, cols] = both
            acc += both.astype(F32)
        sums = jnp.sum(acc, axis=1, keepdims=True)
        mean_row = jnp.transpose(meanb[tokens, :])[:1, :]
        vbt[i] = dot_nt(xw[...], stored_v[i]) - sums * mean_row

    def copy_c(dn, slot):
        return pltpu.make_async_remote_copy(
            src_ref=red,
            dst_ref=recv_c.at[slot],
            send_sem=send_c.at[dn],
            recv_sem=got_c.at[slot],
            device_id=(c_wide, dn),
            device_id_type=MESH,
        )

    my_c_slot = 2 * img + lax.rem(n, 2)
    total = own[me_b]
    red[...] = total

    @pl.loop(1, 16)
    def _(k):
        t = lax.rem(me_b + k, 16)
        copy_b(t, t, t, b_device(t)).wait_recv()
        red[...] += recv_b[t]

    @pl.loop(1, 9)
    def _(k):
        dn = lax.rem(n + k, 8)

        @pl.when(jnp.logical_or(k < 8, jnp.logical_not(c_self)))
        def _():
            copy_c(dn, my_c_slot).start()

    @pl.when(c_self)
    def _():
        recv_c[my_c_slot] = red[...]

    def copy_m(t, slot):
        return pltpu.make_async_remote_copy(
            src_ref=red_l,
            dst_ref=recv_m.at[slot],
            send_sem=send_m.at[t],
            recv_sem=got_m.at[slot],
            device_id=(w, t),
            device_id_type=MESH,
        )

    red_l[...] = low_part[n]

    @pl.loop(1, 8)
    def _(k):
        t = lax.rem(n + k, 8)
        copy_l(t, t).wait_recv()
        red_l[...] += recv_l[t]

    recv_m[n] = red_l[...]

    @pl.loop(1, 8)
    def _(k):
        copy_m(lax.rem(n + k, 8), n).start()

    @pl.loop(0, 6)
    def _(j):
        weight_copy(j).wait()
        rows = pl.ds(pl.multiple_of(j * 256, 256), 256)
        nz[j] = dot_nt(zp[...], weight_v[rows, :])

    put = dot_nt(u_ref[...], zp[1024:1280, :])

    @pl.loop(0, 8)
    def _(k):
        sw, sn = 4 * lax.div(k, 2) + grp, 2 * img + lax.rem(k, 2)

        @pl.when(jnp.logical_or(sw != w, sn != n))
        def _():
            copy_c(0, k).wait_recv()

    @pl.loop(1, 8)
    def _(k):
        t = lax.rem(n + k, 8)
        copy_m(t, t).wait_recv()

    t1 = []
    for i in range(4):
        tok = slice(256 * i, 256 * i + 256)
        lat = jnp.concatenate([recv_c[2 * i], recv_c[2 * i + 1]], 1)
        pat = (lat * VAE_INVERSE).astype(BF16)
        pf = pat.astype(F32)
        inv = jnp.transpose(invb[tok, :])[:1, :]
        vb = vbt[i]
        k_row = inv * inv * (jnp.sum(pf * vb[:64], axis=0, keepdims=True) * (1.0 / D))
        pu = put[:, 64 * i : 64 * i + 64]
        pu_hi = pu.astype(BF16)
        pu_lo = (pu - pu_hi.astype(F32)).astype(BF16)
        back = (inv * (dot_nn(pu_hi, pat) + dot_nn(pu_lo, pat) - k_row * vb[64:])).astype(BF16)
        ip = inv * pf
        ip_hi = ip.astype(BF16)
        ip_lo = (ip - ip_hi.astype(F32)).astype(BF16)
        backt[:, tok] = back
        stack = jnp.concatenate([ip_hi, ip_lo, ip_hi, back], 0)
        ltile[tok, :] = jnp.transpose(stack.astype(F32)).astype(BF16)
        ik = inv * k_row
        ikcol[tok, :] = jnp.transpose(jnp.broadcast_to(ik, (128, 256)))
        low = (jnp.concatenate([recv_m[2 * i], recv_m[2 * i + 1]], 1) * NORM).astype(BF16)
        klt[:, tok] = (-ik * low.astype(F32)).astype(BF16)
        t1.append(dot_nt(low, ip_hi) + dot_nt(low, ip_lo))
    klt[:, 1024:1280] = jnp.concatenate(t1, 1).astype(BF16)

    up_t = dot_nn(klt[...], zp[:, pl.ds(pl.multiple_of(n * 384, 128), 384)])
    ubuf[0] = up_t[:, :256]
    ubuf[1] = pltpu.roll(up_t[:, 128:384], 192, 1)

    def copy_u(t, slot):
        return pltpu.make_async_remote_copy(
            src_ref=ubuf.at[lax.div(t, 8), pl.ds(pl.multiple_of(lax.rem(t, 8) * 8, 8), 8)],
            dst_ref=recv_u.at[slot],
            send_sem=send_u.at[t],
            recv_sem=got_u.at[slot],
            device_id=(t, n),
            device_id_type=MESH,
        )

    @pl.loop(1, 16)
    def _(k):
        copy_u(lax.rem(w + k, 16), w).start()

    down_t = dot_nn(backt[...], hid[...]) * NORM
    for t in range(16):
        first = 96 * t // 128 * 128
        off = 96 * t - first
        if off + 96 <= 128:
            piece = down_t[:, first : first + 128]
            piece = pltpu.roll(piece, 128 - off, 1) if off else piece
        else:
            piece = pltpu.roll(down_t[:, first : first + 256], 256 - off, 1)[:, :128]
        dbuf[t] = piece

    def copy_d(t, slot):
        return pltpu.make_async_remote_copy(
            src_ref=dbuf.at[t],
            dst_ref=recv_d.at[slot],
            send_sem=send_d.at[t],
            recv_sem=got_d.at[slot],
            device_id=(t, n),
            device_id_type=MESH,
        )

    @pl.loop(1, 16)
    def _(k):
        copy_d(lax.rem(w + k, 16), w).start()

    @pl.loop(0, 4)
    def _(i):
        rows = pl.ds(pl.multiple_of(i * 256, 256), 256)
        for j in range(6):
            cols = slice(256 * j, 256 * j + 256)
            q = nz[j, pl.ds(pl.multiple_of(1024 + 64 * i, 64), 64), :]
            q_hi = q.astype(BF16)
            q_lo = (q - q_hi.astype(F32)).astype(BF16)
            right = jnp.concatenate([q_hi, q_hi, q_lo, at_ref[:, cols]], 0)
            prod[...] = dot_nn(ltile[rows, :], right)
            for r in range(8):
                here = pl.ds(pl.multiple_of(i * 256 + r * 32, 32), 32)
                m = pre_v[i, 32 * r : 32 * r + 32, cols].astype(F32)
                sq = m * m
                h = 0.5 + 0.5 * jnp.tanh(m * (GELU_A + (GELU_A * 0.044715) * sq))
                slope = h + (2.0 * m) * h * (1.0 - h) * (GELU_A + (GELU_A * 0.134145) * sq)
                coef = ikcol[here, :]
                grad = prod[32 * r : 32 * r + 32, :] - jnp.concatenate([coef, coef], 1) * nz[j, here, :]
                pre_v[i, 32 * r : 32 * r + 32, cols] = (grad * slope).astype(BF16)
        out_copy(i).start()

    def copy_e(dn, slot):
        return pltpu.make_async_remote_copy(
            src_ref=red_u,
            dst_ref=recv_e.at[slot],
            send_sem=send_e.at[dn],
            recv_sem=got_e.at[slot],
            device_id=(e_wide, dn),
            device_id_type=MESH,
        )

    my_e_slot = lax.rem(w, 8)
    red_u[...] = ubuf[lax.div(w, 8), pl.ds(pl.multiple_of(my_e_slot * 8, 8), 8)]

    @pl.loop(1, 16)
    def _(k):
        t = lax.rem(w + k, 16)
        copy_u(t, t).wait_recv()
        red_u[...] += recv_u[t]

    @pl.loop(1, 9)
    def _(k):
        dn = lax.rem(n + k, 8)

        @pl.when(jnp.logical_or(k < 8, jnp.logical_not(e_self)))
        def _():
            copy_e(dn, my_e_slot).start()

    @pl.when(e_self)
    def _():
        recv_e[my_e_slot] = red_u[...]

    recv_d[w] = dbuf[w]

    @pl.loop(1, 16)
    def _(k):
        t = lax.rem(w + k, 16)
        copy_d(t, t).wait_recv()

    down = recv_d[0]
    for t in range(1, 16):
        down = down + recv_d[t]
    down_out[...] = down[:, :96]

    @pl.loop(0, 8)
    def _(k):
        @pl.when(jnp.logical_or(8 * core + k != w, lax.div(w, 2) != n))
        def _():
            copy_e(0, k).wait_recv()

    up = jnp.concatenate([recv_e[k] for k in range(8)], 0)
    up_out[...] = up[:, :192]

    @pl.loop(1, 16)
    def _(k):
        t = lax.rem(me_b + k, 16)
        copy_b(t, t, t, b_device(t)).wait_send()
        t = lax.rem(w + k, 16)
        copy_u(t, t).wait_send()
        copy_d(t, t).wait_send()

    @pl.loop(1, 9)
    def _(k):
        dn = lax.rem(n + k, 8)

        @pl.when(k < 8)
        def _():
            copy_l(dn, n).wait_send()
            copy_m(dn, n).wait_send()

        @pl.when(jnp.logical_or(k < 8, jnp.logical_not(c_self)))
        def _():
            copy_c(dn, my_c_slot).wait_send()

        @pl.when(jnp.logical_or(k < 8, jnp.logical_not(e_self)))
        def _():
            copy_e(dn, my_e_slot).wait_send()

    @pl.loop(0, 4)
    def _(i):
        out_copy(i).wait()


def main(*args):
    dma = pltpu.SemaphoreType.DMA
    v = pltpu.VMEM
    anywhere = pl.BlockSpec(memory_space=pl.ANY)
    vmem = pl.BlockSpec(memory_space=pltpu.VMEM)
    return pl.pallas_call(
        main_kernel,
        out_shape=(
            jax.ShapeDtypeStruct((4, 256, F), BF16),
            jax.ShapeDtypeStruct((64, 192), F32),
            jax.ShapeDtypeStruct((64, 96), F32),
        ),
        in_specs=[anywhere] * 10,
        out_specs=(anywhere, vmem, vmem),
        scratch_shapes=[
            v((16, 64, 128), F32),
            v((16, 64, 128), F32),
            v((16, 64, 128), F32),
            v((16, 64, 128), F32),
            v((64, 128), F32),
            v((8, 64, 128), F32),
            v((8, 64, 128), F32),
            v((8, 64, 128), F32),
            v((64, 128), F32),
            v((8, 64, 128), F32),
            v((2, 64, 256), F32),
            v((16, 8, 256), F32),
            v((8, 256), F32),
            v((8, 8, 256), F32),
            v((16, 64, 128), F32),
            v((16, 64, 128), F32),
            v((4, 256, D), BF16),
            v((4, 256, F), BF16),
            v((F, D), BF16),
            v((1280, D), BF16),
            v((128, D), BF16),
            v((1024, F), BF16),
            v((6, 1280, 256), F32),
            v((256, 256), F32),
            v((16, 128, 128), BF16),
            v((144, 512), BF16),
            v((4, 130, 16, 128), BF16),
            v((64, D), BF16),
            v((64, D), BF16),
            v((4, D), BF16),
            v((4, D), BF16),
            v((1024, 128), F32),
            v((1024, 128), F32),
            v((4, 128, 256), F32),
            v((1024, 128), F32),
            v((1024, 256), BF16),
            v((64, 1024), BF16),
            v((64, 1280), BF16),
            v((64, F), BF16),
            v((4, 8, D), F32),
            v((4, 8, D), F32),
            dma((7,)),
            dma((4,)),
            dma((4,)),
            dma((6,)),
            dma((4,)),
            dma((1,)),
            dma((1,)),
            dma((16,)),
            dma((16,)),
            dma((8,)),
            dma((8,)),
            dma((8,)),
            dma((8,)),
            dma((8,)),
            dma((8,)),
            dma((16,)),
            dma((16,)),
            dma((8,)),
            dma((8,)),
            dma((16,)),
            dma((16,)),
        ],
        compiler_params=pltpu.CompilerParams(
            collective_id=0, has_side_effects=True, vmem_limit_bytes=60 * MIB
        ),
        name="main",
    )(*args)


def local(
    cotangent,
    decoder_kernel,
    patch_projection_rows,
    stored_hidden_state,
    output_norm_scale,
    output_gate,
    preactivation_input,
    frozen_down_weight,
    adapter_down_rows,
    adapter_up_rows,
):
    pre_grad, up_grad, down_grad = main(
        cotangent[0],
        decoder_kernel.transpose(1, 2, 0).reshape(144, 512),
        stored_hidden_state,
        preactivation_input,
        frozen_down_weight,
        adapter_down_rows.T,
        adapter_up_rows,
        patch_projection_rows,
        output_norm_scale,
        output_gate,
    )
    return pre_grad, up_grad.T, down_grad.T


def solution(mesh):
    placed = (
        P("wide", "narrow", None, None),
        P(),
        P(),
        P(None, "wide", None),
        P(),
        P(),
        P(None, "wide", "narrow"),
        P("narrow", None),
        P("narrow", None),
        P(),
    )
    return jax.shard_map(
        local,
        mesh=mesh,
        in_specs=placed,
        out_specs=(P(None, "wide", "narrow"), P("wide", None), P(("narrow", "wide"), None)),
        check_vma=False,
    )
```

```python
import jax
import jax.numpy as jnp
from jax import lax
from jax.experimental import pallas as pl
from jax.experimental.pallas import tpu as pltpu
from jax.sharding import PartitionSpec as P

MESH = pl.DeviceIdType.MESH
F32 = jnp.float32
BF16 = jnp.bfloat16
D = 3072
F = 1536
VAE_INVERSE = 1.0 / 0.3611
NORM = 1.0 / 128.0
GELU_A = 0.7978845608
MIB = 1 << 20


def dot_nt(a, b):
    return lax.dot_general(a, b, (((1,), (1,)), ((), ())), preferred_element_type=F32)


def dot_nn(a, b):
    return lax.dot_general(a, b, (((1,), (0,)), ((), ())), preferred_element_type=F32)


def dot_tn(a, b):
    return lax.dot_general(a, b, (((0,), (0,)), ((), ())), preferred_element_type=F32)


def iota(shape, axis):
    return lax.broadcasted_iota(jnp.int32, shape, axis)


def one_hot(mask):
    return mask.astype(F32).astype(BF16)


def column_taps():
    col = iota((128, 512), 1)
    return one_hot(iota((128, 512), 0) == 2 * (col & 63) - 1 + (col >> 7))


def kernel_taps():
    col = iota((16, 1024), 1)
    same = iota((16, 1024), 0) == (col & 63) >> 2
    dy = ((col >> 1) & 1) + 2 - (col >> 8)
    dx = (col & 1) + 2 - ((col >> 6) & 3)
    return jnp.concatenate(
        [one_hot(same & (dy == t // 3) & (dx == t % 3)) for t in range(9)], 0
    )


def main_kernel(
    cot,
    taps_in,
    stored,
    pre,
    weight,
    a_in,
    u_in,
    p_in,
    scale_in,
    gate_in,
    pre_out,
    up_out,
    down_out,
    own,
    recv_a,
    recv_b,
    red,
    recv_c,
    low_part,
    recv_l,
    red_l,
    recv_m,
    ubuf,
    recv_u,
    red_u,
    recv_e,
    dbuf,
    recv_d,
    stored_v,
    pre_v,
    weight_v,
    z0,
    z1,
    z2,
    z3,
    pc,
    xw0,
    xw1,
    hid,
    slope,
    nz,
    prod0,
    prod1,
    cot_v,
    taps_v,
    g_ref,
    u_ref,
    p_ref,
    scale_ref,
    gate_ref,
    meanb,
    invb,
    vbt,
    ikcol,
    ltile,
    backt,
    klt,
    at_ref,
    gate_v,
    scale_v,
    sem_local,
    sem_pre,
    sem_stored,
    sem_weight,
    sem_out,
    send_a,
    got_a,
    send_b,
    got_b,
    send_c,
    got_c,
    send_l,
    got_l,
    send_m,
    got_m,
    send_u,
    got_u,
    send_e,
    got_e,
    send_d,
    got_d,
):
    zps = (z0, z1, z2, z3)
    xws = (xw0, xw1)
    prods = (prod0, prod1)
    w = lax.axis_index("wide")
    n = lax.axis_index("narrow")
    img = lax.div(w, 4)
    grp = lax.rem(w, 4)
    core = lax.rem(w, 2)
    me_b = lax.div(grp, 2) * 8 + n
    c_wide = 4 * lax.div(n, 2) + grp
    e_wide = 2 * n + lax.div(w, 8)
    c_self = c_wide == w
    e_self = e_wide == w

    small = [
        pltpu.make_async_copy(src, dst, sem_local.at[k])
        for k, (src, dst) in enumerate(
            [
                (cot, cot_v),
                (taps_in, taps_v),
                (a_in, at_ref),
                (gate_in, gate_ref),
                (scale_in, scale_ref),
                (p_in, p_ref),
                (u_in, u_ref),
            ]
        )
    ]
    for copy in small:
        copy.start()

    def pre_copy(i):
        return pltpu.make_async_copy(pre.at[i], pre_v.at[i], sem_pre.at[i])

    def stored_copy(i):
        return pltpu.make_async_copy(stored.at[i], stored_v.at[i], sem_stored.at[i])

    def weight_copy(j):
        rows = pl.ds(pl.multiple_of(j * 256, 256), 256)
        return pltpu.make_async_copy(weight.at[rows], weight_v.at[rows], sem_weight.at[j])

    def out_copy(i):
        return pltpu.make_async_copy(pre_v.at[i], pre_out.at[i], sem_out.at[i])

    stored_copy(0).start()

    @pl.loop(0, 6)
    def _(j):
        weight_copy(j).start()

    stored_copy(1).start()

    @pl.loop(0, 4)
    def _(i):
        pre_copy(i).start()

    stored_copy(2).start()
    stored_copy(3).start()

    barrier = pltpu.get_barrier_semaphore()

    def greet(dw, dn):
        pl.semaphore_signal(barrier, inc=1, device_id=(dw, dn), device_id_type=MESH)

    def b_device(t):
        return 4 * img + 2 * lax.div(t, 8) + core, lax.rem(t, 8)

    @pl.loop(1, 16)
    def _(k):
        greet(*b_device(lax.rem(me_b + k, 16)))
        greet(lax.rem(w + k, 16), n)

    @pl.loop(0, 8)
    def _(k):
        cw, cn = 4 * lax.div(k, 2) + grp, 2 * img + lax.rem(k, 2)

        @pl.when(jnp.logical_or(cw != w, cn != n))
        def _():
            greet(cw, cn)

        ew, en = 8 * core + k, lax.div(w, 2)

        @pl.when(jnp.logical_or(ew != w, en != n))
        def _():
            greet(ew, en)

    zero = jnp.zeros((16, 128), BF16)
    for tap in range(4):
        g_ref[tap, 0] = zero
        g_ref[tap, 129] = zero
    columns = column_taps()
    routes = kernel_taps()
    small[0].wait()

    @pl.loop(0, 4)
    def _(r):
        rows = cot_v[:, pl.ds(pl.multiple_of(r * 32, 32), 32), :]
        moved = dot_nn(jnp.swapaxes(rows, 0, 1).reshape(512, 128), columns)
        for tap in range(4):
            g_ref[tap, pl.ds(1 + r * 32, 32)] = (
                moved[:, 128 * tap : 128 * tap + 128].astype(BF16).reshape(32, 16, 128)
            )

    small[1].wait()
    pick = one_hot(iota((16, 512), 1) - grp * 128 - n * 16 == iota((16, 512), 0))
    mine = dot_nn(dot_nt(pick, taps_v[...]).astype(BF16), routes)
    mine = jnp.concatenate([mine[:, 64 * t : 64 * t + 64] for t in range(16)], 0)
    weights = jnp.transpose(mine).astype(BF16)
    left_half = iota((16, 128), 1) < 64

    def conv(side, dst):
        @pl.loop(0, 4)
        def _(quarter):
            for z in range(2):
                for half in range(2):
                    row = 32 * quarter + 16 * z + 8 * side + 4 * half
                    window = [
                        jnp.where(left_half, g_ref[tx, row + ty], g_ref[tx, row + 2 + ty])
                        for ty in range(4)
                        for tx in range(4)
                    ]
                    dst[8 * z + 2 * quarter + half] = dot_nn(
                        weights, jnp.concatenate(window, 0)
                    )

    conv(1 - core, dbuf)
    pl.semaphore_wait(barrier, 46 - c_self.astype(jnp.int32) - e_self.astype(jnp.int32))

    copy_a = pltpu.make_async_remote_copy(
        src_ref=dbuf,
        dst_ref=recv_a,
        send_sem=send_a.at[0],
        recv_sem=got_a.at[0],
        device_id=(w + 1 - 2 * core, n),
        device_id_type=MESH,
    )
    copy_a.start()
    conv(core, own)
    for copy in small[2:]:
        copy.wait()

    def copy_b(src, slot, t, dev):
        return pltpu.make_async_remote_copy(
            src_ref=own.at[src],
            dst_ref=recv_b.at[slot],
            send_sem=send_b.at[t],
            recv_sem=got_b.at[slot],
            device_id=dev,
            device_id_type=MESH,
        )

    def start_b():
        copy_a.wait()

        @pl.loop(1, 17)
        def _(k):
            t = lax.rem(me_b + k, 16)
            own[t] = own[t] + recv_a[t]

            @pl.when(k < 16)
            def _():
                copy_b(t, me_b, t, b_device(t)).start()

    gates = gate_ref[...].astype(F32)
    scales = 1.0 + scale_ref[...].astype(F32)
    for i in range(4):
        gate_v[i] = jnp.broadcast_to(gates[i : i + 1], (8, D))
        scale_v[i] = jnp.broadcast_to(scales[i : i + 1], (8, D))

    def stats(i):
        @pl.loop(0, 16, unroll=16)
        def _(r):
            acc = jnp.zeros((16, 128), F32)
            for s in range(24):
                cols = slice(128 * s, 128 * s + 128)
                acc += stored_v[i, pl.ds(r * 16, 16), cols].astype(F32)
            meanb[pl.ds(i * 256 + r * 16, 16), :] = acc

        tokens = slice(256 * i, 256 * i + 256)
        mean = jnp.sum(meanb[tokens, :], axis=1, keepdims=True) * (1.0 / D)
        meanb[tokens, :] = jnp.broadcast_to(mean, (256, 128))

        @pl.loop(0, 16, unroll=16)
        def _(r):
            here = pl.ds(i * 256 + r * 16, 16)
            mean = meanb[here, :]
            acc = jnp.zeros((16, 128), F32)
            for s in range(24):
                cols = slice(128 * s, 128 * s + 128)
                x = stored_v[i, pl.ds(r * 16, 16), cols].astype(F32) - mean
                zps[i][pl.ds(r * 16, 16), cols] = (x * gate_v[i, 0:1, cols]).astype(BF16)
                acc += x * x
            invb[here, :] = acc

        var = jnp.sum(invb[tokens, :], axis=1, keepdims=True) * (1.0 / D)
        invb[tokens, :] = jnp.broadcast_to(1.0 / jnp.sqrt(var + 1e-06), (256, 128))

    def prep(i):
        def total(s, acc):
            cols = pl.ds(128 * s, 128)
            return acc + p_ref[:, cols].astype(F32) * scale_v[i, 0:1, cols]

        acc = lax.fori_loop(0, 24, total, jnp.zeros((64, 128), F32), unroll=24)
        mean = jnp.broadcast_to(jnp.sum(acc, axis=1, keepdims=True) * (1.0 / D), (64, 128))

        def fill(s, acc):
            cols = pl.ds(128 * s, 128)
            gate = gate_v[i, 0:1, cols]
            x = p_ref[:, cols].astype(F32) * scale_v[i, 0:1, cols] - mean
            pc[64 * i : 64 * i + 64, cols] = (x * gate).astype(BF16)
            both = jnp.concatenate([x, u_ref[:, cols].astype(F32) * gate], 0).astype(BF16)
            xws[i % 2][:, cols] = both
            return acc + both.astype(F32)

        acc = lax.fori_loop(0, 24, fill, jnp.zeros((128, 128), F32), unroll=24)
        return jnp.sum(acc, axis=1, keepdims=True)

    def large(i):
        nz[256 * i : 256 * i + 256, :] = dot_nt(zps[i][...], weight_v[...])

    def small_products(i, sums):
        tokens = slice(256 * i, 256 * i + 256)
        mean_row = jnp.transpose(meanb[tokens, :])[:1, :]
        vbt[i] = dot_nt(xws[i % 2][...], stored_v[i]) - sums * mean_row

    def gelu(i):
        @pl.loop(0, 16, unroll=16)
        def _(r):
            rows = pl.ds(r * 16, 16)
            here = pl.ds(i * 256 + r * 16, 16)
            for s in range(3):
                cols = slice(512 * s, 512 * s + 512)
                m = pre_v[i, rows, cols].astype(F32)
                h = 0.5 + 0.5 * jnp.tanh(m * (GELU_A + (GELU_A * 0.044715) * (m * m)))
                hid[here, cols] = (m * h).astype(BF16)

    def slopes(i):
        @pl.loop(0, 16, unroll=16)
        def _(r):
            rows = pl.ds(r * 16, 16)
            here = pl.ds(i * 256 + r * 16, 16)
            for s in range(3):
                cols = slice(512 * s, 512 * s + 512)
                m = pre_v[i, rows, cols].astype(F32)
                sq = m * m
                h = 0.5 + 0.5 * jnp.tanh(m * (GELU_A + (GELU_A * 0.044715) * sq))
                slope[here, cols] = h + (2.0 * m) * h * (1.0 - h) * (
                    GELU_A + (GELU_A * 0.134145) * sq
                )

    stored_copy(0).wait()
    sums = prep(0)
    stats(0)
    start_b()

    def copy_l(t, slot):
        return pltpu.make_async_remote_copy(
            src_ref=low_part.at[t],
            dst_ref=recv_l.at[slot],
            send_sem=send_l.at[t],
            recv_sem=got_l.at[slot],
            device_id=(w, t),
            device_id_type=MESH,
        )

    @pl.loop(0, 6)
    def _(j):
        weight_copy(j).wait()

    stored_copy(1).wait()
    for i in range(4):
        pre_copy(i).wait()
    large(0)
    small_products(0, sums)
    stats(1)
    sums = prep(1)
    for i in range(4):
        gelu(i)
    for i in range(4):
        lt = dot_nt(at_ref[...], hid[256 * i : 256 * i + 256, :])
        low_part[2 * i] = lt[:, :128]
        low_part[2 * i + 1] = lt[:, 128:]

    @pl.loop(1, 8)
    def _(k):
        copy_l(lax.rem(n + k, 8), n).start()

    stored_copy(2).wait()
    large(1)
    small_products(1, sums)
    stats(2)
    sums = prep(2)

    def copy_c(dn, slot):
        return pltpu.make_async_remote_copy(
            src_ref=red,
            dst_ref=recv_c.at[slot],
            send_sem=send_c.at[dn],
            recv_sem=got_c.at[slot],
            device_id=(c_wide, dn),
            device_id_type=MESH,
        )

    my_c_slot = 2 * img + lax.rem(n, 2)
    total = own[me_b]
    red[...] = total

    @pl.loop(1, 16)
    def _(k):
        t = lax.rem(me_b + k, 16)
        copy_b(t, t, t, b_device(t)).wait_recv()
        red[...] += recv_b[t]

    @pl.loop(1, 9)
    def _(k):
        dn = lax.rem(n + k, 8)

        @pl.when(jnp.logical_or(k < 8, jnp.logical_not(c_self)))
        def _():
            copy_c(dn, my_c_slot).start()

    @pl.when(c_self)
    def _():
        recv_c[my_c_slot] = red[...]

    def copy_m(t, slot):
        return pltpu.make_async_remote_copy(
            src_ref=red_l,
            dst_ref=recv_m.at[slot],
            send_sem=send_m.at[t],
            recv_sem=got_m.at[slot],
            device_id=(w, t),
            device_id_type=MESH,
        )

    red_l[...] = low_part[n]

    @pl.loop(1, 8)
    def _(k):
        t = lax.rem(n + k, 8)
        copy_l(t, t).wait_recv()
        red_l[...] += recv_l[t]

    recv_m[n] = red_l[...]

    @pl.loop(1, 8)
    def _(k):
        copy_m(lax.rem(n + k, 8), n).start()

    stored_copy(3).wait()
    large(2)
    small_products(2, sums)
    stats(3)
    sums = prep(3)
    slopes(0)
    slopes(1)
    small_products(3, sums)
    put = dot_nt(u_ref[...], pc[...])

    @pl.loop(0, 8)
    def _(k):
        sw, sn = 4 * lax.div(k, 2) + grp, 2 * img + lax.rem(k, 2)

        @pl.when(jnp.logical_or(sw != w, sn != n))
        def _():
            copy_c(0, k).wait_recv()

    @pl.loop(1, 8)
    def _(k):
        t = lax.rem(n + k, 8)
        copy_m(t, t).wait_recv()

    t1 = []
    for i in range(4):
        tok = slice(256 * i, 256 * i + 256)
        lat = jnp.concatenate([recv_c[2 * i], recv_c[2 * i + 1]], 1)
        pat = (lat * VAE_INVERSE).astype(BF16)
        pf = pat.astype(F32)
        inv = jnp.transpose(invb[tok, :])[:1, :]
        vb = vbt[i]
        k_row = inv * inv * (jnp.sum(pf * vb[:64], axis=0, keepdims=True) * (1.0 / D))
        pu = put[:, 64 * i : 64 * i + 64]
        pu_hi = pu.astype(BF16)
        pu_lo = (pu - pu_hi.astype(F32)).astype(BF16)
        back = (inv * (dot_nn(pu_hi, pat) + dot_nn(pu_lo, pat) - k_row * vb[64:])).astype(BF16)
        ip = inv * pf
        ip_hi = ip.astype(BF16)
        ip_lo = (ip - ip_hi.astype(F32)).astype(BF16)
        backt[:, tok] = back
        stack = jnp.concatenate([ip_hi, ip_lo, ip_hi, back], 0)
        ltile[tok, :] = jnp.transpose(stack.astype(F32)).astype(BF16)
        ik = inv * k_row
        ikcol[tok, :] = jnp.transpose(jnp.broadcast_to(ik, (128, 256)))
        low = (jnp.concatenate([recv_m[2 * i], recv_m[2 * i + 1]], 1) * NORM).astype(BF16)
        klt[:, tok] = (-ik * low.astype(F32)).astype(BF16)
        t1.append(dot_nt(low, ip_hi) + dot_nt(low, ip_lo))
    klt[:, 1024:1280] = jnp.concatenate(t1, 1).astype(BF16)

    mine = pl.ds(pl.multiple_of(n * 384, 128), 384)
    up_t = dot_nn(klt[:, 1024:1280], pc[:, mine])
    for i in range(4):
        up_t += dot_nn(klt[:, 256 * i : 256 * i + 256], zps[i][:, mine])
    ubuf[0] = up_t[:, :256]
    ubuf[1] = pltpu.roll(up_t[:, 128:384], 192, 1)

    def copy_u(t, slot):
        return pltpu.make_async_remote_copy(
            src_ref=ubuf.at[lax.div(t, 8), pl.ds(pl.multiple_of(lax.rem(t, 8) * 8, 8), 8)],
            dst_ref=recv_u.at[slot],
            send_sem=send_u.at[t],
            recv_sem=got_u.at[slot],
            device_id=(t, n),
            device_id_type=MESH,
        )

    @pl.loop(1, 16)
    def _(k):
        copy_u(lax.rem(w + k, 16), w).start()

    down_t = dot_nn(backt[...], hid[...]) * NORM
    for t in range(16):
        first = 96 * t // 128 * 128
        off = 96 * t - first
        if off + 96 <= 128:
            piece = down_t[:, first : first + 128]
            piece = pltpu.roll(piece, 128 - off, 1) if off else piece
        else:
            piece = pltpu.roll(down_t[:, first : first + 256], 256 - off, 1)[:, :128]
        dbuf[t] = piece

    def copy_d(t, slot):
        return pltpu.make_async_remote_copy(
            src_ref=dbuf.at[t],
            dst_ref=recv_d.at[slot],
            send_sem=send_d.at[t],
            recv_sem=got_d.at[slot],
            device_id=(t, n),
            device_id_type=MESH,
        )

    @pl.loop(1, 16)
    def _(k):
        copy_d(lax.rem(w + k, 16), w).start()

    large(3)
    slopes(2)
    slopes(3)

    def copy_e(dn, slot):
        return pltpu.make_async_remote_copy(
            src_ref=red_u,
            dst_ref=recv_e.at[slot],
            send_sem=send_e.at[dn],
            recv_sem=got_e.at[slot],
            device_id=(e_wide, dn),
            device_id_type=MESH,
        )

    my_e_slot = lax.rem(w, 8)
    red_u[...] = ubuf[lax.div(w, 8), pl.ds(pl.multiple_of(my_e_slot * 8, 8), 8)]

    @pl.loop(1, 16)
    def _(k):
        t = lax.rem(w + k, 16)
        copy_u(t, t).wait_recv()
        red_u[...] += recv_u[t]

    @pl.loop(1, 9)
    def _(k):
        dn = lax.rem(n + k, 8)

        @pl.when(jnp.logical_or(k < 8, jnp.logical_not(e_self)))
        def _():
            copy_e(dn, my_e_slot).start()

    @pl.when(e_self)
    def _():
        recv_e[my_e_slot] = red_u[...]

    nz[1024:1280, :] = dot_nt(pc[...], weight_v[...])

    def grads(i, h):
        cols = slice(768 * h, 768 * h + 768)
        q = nz[1024 + 64 * i : 1088 + 64 * i, cols]
        q_hi = q.astype(BF16)
        q_lo = (q - q_hi.astype(F32)).astype(BF16)
        right = jnp.concatenate([q_hi, q_hi, q_lo, at_ref[:, cols]], 0)
        prods[h][...] = dot_nn(ltile[256 * i : 256 * i + 256, :], right)

    def finish(i, h):
        @pl.loop(0, 16, unroll=16)
        def _(r):
            rows = pl.ds(r * 16, 16)
            here = pl.ds(i * 256 + r * 16, 16)
            coef = ikcol[here, :]
            coef = jnp.concatenate([coef] * 3, 1)
            for s in range(2):
                cols = slice(768 * h + 384 * s, 768 * h + 384 * s + 384)
                grad = prods[h][rows, 384 * s : 384 * s + 384] - coef * nz[here, cols]
                pre_v[i, rows, cols] = (grad * slope[here, cols]).astype(BF16)

    grads(0, 0)
    for i in range(4):
        grads(i, 1)
        finish(i, 0)
        if i < 3:
            grads(i + 1, 0)
        finish(i, 1)
        out_copy(i).start()

    recv_d[w] = dbuf[w]

    @pl.loop(1, 16)
    def _(k):
        t = lax.rem(w + k, 16)
        copy_d(t, t).wait_recv()

    down = recv_d[0]
    for t in range(1, 16):
        down = down + recv_d[t]
    down_out[...] = down[:, :96]

    @pl.loop(0, 8)
    def _(k):
        @pl.when(jnp.logical_or(8 * core + k != w, lax.div(w, 2) != n))
        def _():
            copy_e(0, k).wait_recv()

    up = jnp.concatenate([recv_e[k] for k in range(8)], 0)
    up_out[...] = up[:, :192]

    @pl.loop(1, 16)
    def _(k):
        t = lax.rem(me_b + k, 16)
        copy_b(t, t, t, b_device(t)).wait_send()
        t = lax.rem(w + k, 16)
        copy_u(t, t).wait_send()
        copy_d(t, t).wait_send()

    @pl.loop(1, 9)
    def _(k):
        dn = lax.rem(n + k, 8)

        @pl.when(k < 8)
        def _():
            copy_l(dn, n).wait_send()
            copy_m(dn, n).wait_send()

        @pl.when(jnp.logical_or(k < 8, jnp.logical_not(c_self)))
        def _():
            copy_c(dn, my_c_slot).wait_send()

        @pl.when(jnp.logical_or(k < 8, jnp.logical_not(e_self)))
        def _():
            copy_e(dn, my_e_slot).wait_send()

    @pl.loop(0, 4)
    def _(i):
        out_copy(i).wait()


def main(*args):
    dma = pltpu.SemaphoreType.DMA
    v = pltpu.VMEM
    anywhere = pl.BlockSpec(memory_space=pl.ANY)
    vmem = pl.BlockSpec(memory_space=pltpu.VMEM)
    return pl.pallas_call(
        main_kernel,
        out_shape=(
            jax.ShapeDtypeStruct((4, 256, F), BF16),
            jax.ShapeDtypeStruct((64, 192), F32),
            jax.ShapeDtypeStruct((64, 96), F32),
        ),
        in_specs=[anywhere] * 10,
        out_specs=(anywhere, vmem, vmem),
        scratch_shapes=[
            v((16, 64, 128), F32),
            v((16, 64, 128), F32),
            v((16, 64, 128), F32),
            v((64, 128), F32),
            v((8, 64, 128), F32),
            v((8, 64, 128), F32),
            v((8, 64, 128), F32),
            v((64, 128), F32),
            v((8, 64, 128), F32),
            v((2, 64, 256), F32),
            v((16, 8, 256), F32),
            v((8, 256), F32),
            v((8, 8, 256), F32),
            v((16, 64, 128), F32),
            v((16, 64, 128), F32),
            v((4, 256, D), BF16),
            v((4, 256, F), BF16),
            v((F, D), BF16),
            v((256, D), BF16),
            v((256, D), BF16),
            v((256, D), BF16),
            v((256, D), BF16),
            v((256, D), BF16),
            v((128, D), BF16),
            v((128, D), BF16),
            v((1024, F), BF16),
            v((1024, F), F32),
            v((1280, F), F32),
            v((256, F // 2), F32),
            v((256, F // 2), F32),
            v((16, 128, 128), BF16),
            v((144, 512), BF16),
            v((4, 130, 16, 128), BF16),
            v((64, D), BF16),
            v((64, D), BF16),
            v((4, D), BF16),
            v((4, D), BF16),
            v((1024, 128), F32),
            v((1024, 128), F32),
            v((4, 128, 256), F32),
            v((1024, 128), F32),
            v((1024, 256), BF16),
            v((64, 1024), BF16),
            v((64, 1280), BF16),
            v((64, F), BF16),
            v((4, 8, D), F32),
            v((4, 8, D), F32),
            dma((7,)),
            dma((4,)),
            dma((4,)),
            dma((6,)),
            dma((4,)),
            dma((1,)),
            dma((1,)),
            dma((16,)),
            dma((16,)),
            dma((8,)),
            dma((8,)),
            dma((8,)),
            dma((8,)),
            dma((8,)),
            dma((8,)),
            dma((16,)),
            dma((16,)),
            dma((8,)),
            dma((8,)),
            dma((16,)),
            dma((16,)),
        ],
        compiler_params=pltpu.CompilerParams(
            collective_id=0, has_side_effects=True, vmem_limit_bytes=62 * MIB
        ),
        name="main",
    )(*args)


def local(
    cotangent,
    decoder_kernel,
    patch_projection_rows,
    stored_hidden_state,
    output_norm_scale,
    output_gate,
    preactivation_input,
    frozen_down_weight,
    adapter_down_rows,
    adapter_up_rows,
):
    pre_grad, up_grad, down_grad = main(
        cotangent[0],
        decoder_kernel.transpose(1, 2, 0).reshape(144, 512),
        stored_hidden_state,
        preactivation_input,
        frozen_down_weight,
        adapter_down_rows.T,
        adapter_up_rows,
        patch_projection_rows,
        output_norm_scale,
        output_gate,
    )
    return pre_grad, up_grad.T, down_grad.T


def solution(mesh):
    placed = (
        P("wide", "narrow", None, None),
        P(),
        P(),
        P(None, "wide", None),
        P(),
        P(),
        P(None, "wide", "narrow"),
        P("narrow", None),
        P("narrow", None),
        P(),
    )
    return jax.shard_map(
        local,
        mesh=mesh,
        in_specs=placed,
        out_specs=(P(None, "wide", "narrow"), P("wide", None), P(("narrow", "wide"), None)),
        check_vma=False,
    )
```

```python
import jax
import jax.numpy as jnp
from jax import lax
from jax.experimental import pallas as pl
from jax.experimental.pallas import tpu as pltpu
from jax.sharding import PartitionSpec as P

MESH = pl.DeviceIdType.MESH
F32 = jnp.float32
BF16 = jnp.bfloat16
D = 3072
F = 1536
VAE_INVERSE = 1.0 / 0.3611
NORM = 1.0 / 128.0
GELU_A = 0.7978845608
MIB = 1 << 20


def dot_nt(a, b):
    return lax.dot_general(a, b, (((1,), (1,)), ((), ())), preferred_element_type=F32)


def dot_nn(a, b):
    return lax.dot_general(a, b, (((1,), (0,)), ((), ())), preferred_element_type=F32)


def dot_tn(a, b):
    return lax.dot_general(a, b, (((0,), (0,)), ((), ())), preferred_element_type=F32)


def iota(shape, axis):
    return lax.broadcasted_iota(jnp.int32, shape, axis)


def one_hot(mask):
    return mask.astype(F32).astype(BF16)


def column_taps():
    col = iota((128, 512), 1)
    return one_hot(iota((128, 512), 0) == 2 * (col & 63) - 1 + (col >> 7))


def kernel_taps():
    col = iota((16, 1024), 1)
    same = iota((16, 1024), 0) == (col & 63) >> 2
    dy = ((col >> 1) & 1) + 2 - (col >> 8)
    dx = (col & 1) + 2 - ((col >> 6) & 3)
    return jnp.concatenate(
        [one_hot(same & (dy == t // 3) & (dx == t % 3)) for t in range(9)], 0
    )


def main_kernel(
    cot,
    taps_in,
    stored,
    pre,
    weight,
    a_in,
    u_in,
    p_in,
    scale_in,
    gate_in,
    pre_out,
    up_out,
    down_out,
    own,
    recv_a,
    recv_b,
    red,
    recv_c,
    low_part,
    recv_l,
    red_l,
    recv_m,
    ubuf,
    recv_u,
    red_u,
    recv_e,
    dbuf,
    recv_d,
    stored_v,
    pre_v,
    weight_v,
    z0,
    z1,
    z2,
    z3,
    pc,
    xw0,
    xw1,
    hid,
    slope,
    nz,
    prod0,
    prod1,
    cot_v,
    taps_v,
    g_ref,
    u_ref,
    p_ref,
    scale_ref,
    gate_ref,
    meanb,
    invb,
    vbt,
    ikcol,
    ltile,
    backt,
    klt,
    at_ref,
    gate_v,
    scale_v,
    sem_local,
    sem_pre,
    sem_stored,
    sem_weight,
    sem_out,
    send_a,
    got_a,
    send_b,
    got_b,
    send_c,
    got_c,
    send_l,
    got_l,
    send_m,
    got_m,
    send_u,
    got_u,
    send_e,
    got_e,
    send_d,
    got_d,
):
    zps = (z0, z1, z2, z3)
    xws = (xw0, xw1)
    prods = (prod0, prod1)
    w = lax.axis_index("wide")
    n = lax.axis_index("narrow")
    img = lax.div(w, 4)
    grp = lax.rem(w, 4)
    core = lax.rem(w, 2)
    me_b = lax.div(grp, 2) * 8 + n
    c_wide = 4 * lax.div(n, 2) + grp
    e_wide = 2 * n + lax.div(w, 8)
    c_self = c_wide == w
    e_self = e_wide == w

    small = [
        pltpu.make_async_copy(src, dst, sem_local.at[k])
        for k, (src, dst) in enumerate(
            [
                (cot, cot_v),
                (taps_in, taps_v),
                (a_in, at_ref),
                (gate_in, gate_ref),
                (scale_in, scale_ref),
                (p_in, p_ref),
                (u_in, u_ref),
            ]
        )
    ]
    for copy in small:
        copy.start()

    def pre_copy(i):
        return pltpu.make_async_copy(pre.at[i], pre_v.at[i], sem_pre.at[i])

    def stored_copy(i):
        return pltpu.make_async_copy(stored.at[i], stored_v.at[i], sem_stored.at[i])

    def weight_copy(j):
        rows = pl.ds(pl.multiple_of(j * 256, 256), 256)
        return pltpu.make_async_copy(weight.at[rows], weight_v.at[rows], sem_weight.at[j])

    def out_copy(i):
        return pltpu.make_async_copy(pre_v.at[i], pre_out.at[i], sem_out.at[i])

    stored_copy(0).start()

    @pl.loop(0, 6)
    def _(j):
        weight_copy(j).start()

    stored_copy(1).start()

    @pl.loop(0, 4)
    def _(i):
        pre_copy(i).start()

    stored_copy(2).start()
    stored_copy(3).start()

    barrier = pltpu.get_barrier_semaphore()

    def greet(dw, dn):
        pl.semaphore_signal(barrier, inc=1, device_id=(dw, dn), device_id_type=MESH)

    def b_device(t):
        return 4 * img + 2 * lax.div(t, 8) + core, lax.rem(t, 8)

    @pl.loop(1, 16)
    def _(k):
        greet(*b_device(lax.rem(me_b + k, 16)))
        greet(lax.rem(w + k, 16), n)

    @pl.loop(0, 8)
    def _(k):
        cw, cn = 4 * lax.div(k, 2) + grp, 2 * img + lax.rem(k, 2)

        @pl.when(jnp.logical_or(cw != w, cn != n))
        def _():
            greet(cw, cn)

        ew, en = 8 * core + k, lax.div(w, 2)

        @pl.when(jnp.logical_or(ew != w, en != n))
        def _():
            greet(ew, en)

    zero = jnp.zeros((16, 128), BF16)
    for tap in range(4):
        g_ref[tap, 0] = zero
        g_ref[tap, 129] = zero
    columns = column_taps()
    routes = kernel_taps()
    pick = one_hot(iota((16, 512), 1) - grp * 128 - n * 16 == iota((16, 512), 0))
    small[0].wait()
    small[1].wait()
    mine = dot_nn(dot_nt(pick, taps_v[...]).astype(BF16), routes)
    mine = jnp.concatenate([mine[:, 64 * t : 64 * t + 64] for t in range(16)], 0)
    for r in range(4):
        rows = jnp.swapaxes(cot_v[:, 32 * r : 32 * r + 32, :], 0, 1).reshape(512, 128)
        moved = dot_nn(rows, columns).astype(BF16)
        for tap in range(4):
            g_ref[tap, 1 + 32 * r : 33 + 32 * r] = moved[:, 128 * tap : 128 * tap + 128].reshape(
                32, 16, 128
            )

    weights = jnp.transpose(mine).astype(BF16)
    left_half = iota((16, 128), 1) < 64

    def conv(side, dst):
        @pl.loop(0, 4)
        def _(quarter):
            for z in range(2):
                for half in range(2):
                    row = 32 * quarter + 16 * z + 8 * side + 4 * half
                    window = [
                        jnp.where(left_half, g_ref[tx, row + ty], g_ref[tx, row + 2 + ty])
                        for ty in range(4)
                        for tx in range(4)
                    ]
                    dst[8 * z + 2 * quarter + half] = dot_nn(
                        weights, jnp.concatenate(window, 0)
                    )

    conv(1 - core, dbuf)
    pl.semaphore_wait(barrier, 46 - c_self.astype(jnp.int32) - e_self.astype(jnp.int32))

    copy_a = pltpu.make_async_remote_copy(
        src_ref=dbuf,
        dst_ref=recv_a,
        send_sem=send_a.at[0],
        recv_sem=got_a.at[0],
        device_id=(w + 1 - 2 * core, n),
        device_id_type=MESH,
    )
    copy_a.start()
    conv(core, own)
    for copy in small[2:]:
        copy.wait()

    def copy_b(src, slot, t, dev):
        return pltpu.make_async_remote_copy(
            src_ref=own.at[src],
            dst_ref=recv_b.at[slot],
            send_sem=send_b.at[t],
            recv_sem=got_b.at[slot],
            device_id=dev,
            device_id_type=MESH,
        )

    def start_b():
        copy_a.wait()

        @pl.loop(1, 17)
        def _(k):
            t = lax.rem(me_b + k, 16)
            own[t] = own[t] + recv_a[t]

            @pl.when(k < 16)
            def _():
                copy_b(t, me_b, t, b_device(t)).start()

    gates = gate_ref[...].astype(F32)
    scales = 1.0 + scale_ref[...].astype(F32)
    for i in range(4):
        gate_v[i] = jnp.broadcast_to(gates[i : i + 1], (8, D))
        scale_v[i] = jnp.broadcast_to(scales[i : i + 1], (8, D))

    def stats(i):
        @pl.loop(0, 16, unroll=16)
        def _(r):
            acc = jnp.zeros((16, 128), F32)
            for s in range(24):
                cols = slice(128 * s, 128 * s + 128)
                acc += stored_v[i, pl.ds(r * 16, 16), cols].astype(F32)
            meanb[pl.ds(i * 256 + r * 16, 16), :] = acc

        tokens = slice(256 * i, 256 * i + 256)
        mean = jnp.sum(meanb[tokens, :], axis=1, keepdims=True) * (1.0 / D)
        meanb[tokens, :] = jnp.broadcast_to(mean, (256, 128))

        @pl.loop(0, 16, unroll=16)
        def _(r):
            here = pl.ds(i * 256 + r * 16, 16)
            mean = meanb[here, :]
            acc = jnp.zeros((16, 128), F32)
            for s in range(24):
                cols = slice(128 * s, 128 * s + 128)
                x = stored_v[i, pl.ds(r * 16, 16), cols].astype(F32) - mean
                zps[i][pl.ds(r * 16, 16), cols] = (x * gate_v[i, 0:1, cols]).astype(BF16)
                acc += x * x
            invb[here, :] = acc

        var = jnp.sum(invb[tokens, :], axis=1, keepdims=True) * (1.0 / D)
        invb[tokens, :] = jnp.broadcast_to(1.0 / jnp.sqrt(var + 1e-06), (256, 128))

    def prep(i):
        def total(s, acc):
            cols = pl.ds(128 * s, 128)
            return acc + p_ref[:, cols].astype(F32) * scale_v[i, 0:1, cols]

        acc = lax.fori_loop(0, 24, total, jnp.zeros((64, 128), F32), unroll=24)
        mean = jnp.broadcast_to(jnp.sum(acc, axis=1, keepdims=True) * (1.0 / D), (64, 128))

        def fill(s, acc):
            cols = pl.ds(128 * s, 128)
            gate = gate_v[i, 0:1, cols]
            x = p_ref[:, cols].astype(F32) * scale_v[i, 0:1, cols] - mean
            pc[64 * i : 64 * i + 64, cols] = (x * gate).astype(BF16)
            both = jnp.concatenate([x, u_ref[:, cols].astype(F32) * gate], 0).astype(BF16)
            xws[i % 2][:, cols] = both
            return acc + both.astype(F32)

        acc = lax.fori_loop(0, 24, fill, jnp.zeros((128, 128), F32), unroll=24)
        return jnp.sum(acc, axis=1, keepdims=True)

    def large(i):
        nz[256 * i : 256 * i + 256, :] = dot_nt(zps[i][...], weight_v[...])

    def small_products(i, sums):
        tokens = slice(256 * i, 256 * i + 256)
        mean_row = jnp.transpose(meanb[tokens, :])[:1, :]
        vbt[i] = dot_nt(xws[i % 2][...], stored_v[i]) - sums * mean_row

    def gelu(i):
        @pl.loop(0, 16, unroll=16)
        def _(r):
            rows = pl.ds(r * 16, 16)
            here = pl.ds(i * 256 + r * 16, 16)
            for s in range(3):
                cols = slice(512 * s, 512 * s + 512)
                m = pre_v[i, rows, cols].astype(F32)
                h = 0.5 + 0.5 * jnp.tanh(m * (GELU_A + (GELU_A * 0.044715) * (m * m)))
                hid[here, cols] = (m * h).astype(BF16)

    def slopes(i):
        @pl.loop(0, 16, unroll=16)
        def _(r):
            rows = pl.ds(r * 16, 16)
            here = pl.ds(i * 256 + r * 16, 16)
            for s in range(3):
                cols = slice(512 * s, 512 * s + 512)
                m = pre_v[i, rows, cols].astype(F32)
                sq = m * m
                h = 0.5 + 0.5 * jnp.tanh(m * (GELU_A + (GELU_A * 0.044715) * sq))
                slope[here, cols] = h + (2.0 * m) * h * (1.0 - h) * (
                    GELU_A + (GELU_A * 0.134145) * sq
                )

    stored_copy(0).wait()
    sums = prep(0)
    stats(0)
    start_b()

    def copy_l(t, slot):
        return pltpu.make_async_remote_copy(
            src_ref=low_part.at[t],
            dst_ref=recv_l.at[slot],
            send_sem=send_l.at[t],
            recv_sem=got_l.at[slot],
            device_id=(w, t),
            device_id_type=MESH,
        )

    @pl.loop(0, 6)
    def _(j):
        weight_copy(j).wait()

    stored_copy(1).wait()
    for i in range(4):
        pre_copy(i).wait()
    large(0)
    small_products(0, sums)
    stats(1)
    sums = prep(1)
    for i in range(4):
        gelu(i)
    for i in range(4):
        lt = dot_nt(at_ref[...], hid[256 * i : 256 * i + 256, :])
        low_part[2 * i] = lt[:, :128]
        low_part[2 * i + 1] = lt[:, 128:]

    @pl.loop(1, 8)
    def _(k):
        copy_l(lax.rem(n + k, 8), n).start()

    stored_copy(2).wait()
    large(1)
    small_products(1, sums)
    stats(2)
    sums = prep(2)

    def copy_c(dn, slot):
        return pltpu.make_async_remote_copy(
            src_ref=red,
            dst_ref=recv_c.at[slot],
            send_sem=send_c.at[dn],
            recv_sem=got_c.at[slot],
            device_id=(c_wide, dn),
            device_id_type=MESH,
        )

    my_c_slot = 2 * img + lax.rem(n, 2)
    total = own[me_b]
    red[...] = total

    @pl.loop(1, 16)
    def _(k):
        t = lax.rem(me_b + k, 16)
        copy_b(t, t, t, b_device(t)).wait_recv()
        red[...] += recv_b[t]

    @pl.loop(1, 9)
    def _(k):
        dn = lax.rem(n + k, 8)

        @pl.when(jnp.logical_or(k < 8, jnp.logical_not(c_self)))
        def _():
            copy_c(dn, my_c_slot).start()

    @pl.when(c_self)
    def _():
        recv_c[my_c_slot] = red[...]

    def copy_m(t, slot):
        return pltpu.make_async_remote_copy(
            src_ref=red_l,
            dst_ref=recv_m.at[slot],
            send_sem=send_m.at[t],
            recv_sem=got_m.at[slot],
            device_id=(w, t),
            device_id_type=MESH,
        )

    red_l[...] = low_part[n]

    @pl.loop(1, 8)
    def _(k):
        t = lax.rem(n + k, 8)
        copy_l(t, t).wait_recv()
        red_l[...] += recv_l[t]

    recv_m[n] = red_l[...]

    @pl.loop(1, 8)
    def _(k):
        copy_m(lax.rem(n + k, 8), n).start()

    stored_copy(3).wait()
    large(2)
    small_products(2, sums)
    stats(3)
    sums = prep(3)
    slopes(0)
    slopes(1)
    small_products(3, sums)
    put = dot_nt(u_ref[...], pc[...])

    @pl.loop(0, 8)
    def _(k):
        sw, sn = 4 * lax.div(k, 2) + grp, 2 * img + lax.rem(k, 2)

        @pl.when(jnp.logical_or(sw != w, sn != n))
        def _():
            copy_c(0, k).wait_recv()

    @pl.loop(1, 8)
    def _(k):
        t = lax.rem(n + k, 8)
        copy_m(t, t).wait_recv()

    t1 = []
    for i in range(4):
        tok = slice(256 * i, 256 * i + 256)
        lat = jnp.concatenate([recv_c[2 * i], recv_c[2 * i + 1]], 1)
        pat = (lat * VAE_INVERSE).astype(BF16)
        pf = pat.astype(F32)
        inv = jnp.transpose(invb[tok, :])[:1, :]
        vb = vbt[i]
        k_row = inv * inv * (jnp.sum(pf * vb[:64], axis=0, keepdims=True) * (1.0 / D))
        pu = put[:, 64 * i : 64 * i + 64]
        pu_hi = pu.astype(BF16)
        pu_lo = (pu - pu_hi.astype(F32)).astype(BF16)
        back = (inv * (dot_nn(pu_hi, pat) + dot_nn(pu_lo, pat) - k_row * vb[64:])).astype(BF16)
        ip = inv * pf
        ip_hi = ip.astype(BF16)
        ip_lo = (ip - ip_hi.astype(F32)).astype(BF16)
        backt[:, tok] = back
        stack = jnp.concatenate([ip_hi, ip_lo, ip_hi, back], 0)
        ltile[tok, :] = jnp.transpose(stack.astype(F32)).astype(BF16)
        ik = inv * k_row
        ikcol[tok, :] = jnp.transpose(jnp.broadcast_to(ik, (128, 256)))
        low = (jnp.concatenate([recv_m[2 * i], recv_m[2 * i + 1]], 1) * NORM).astype(BF16)
        klt[:, tok] = (-ik * low.astype(F32)).astype(BF16)
        t1.append(dot_nt(low, ip_hi) + dot_nt(low, ip_lo))
    klt[:, 1024:1280] = jnp.concatenate(t1, 1).astype(BF16)

    mine = pl.ds(pl.multiple_of(n * 384, 128), 384)
    up_t = dot_nn(klt[:, 1024:1280], pc[:, mine])
    for i in range(4):
        up_t += dot_nn(klt[:, 256 * i : 256 * i + 256], zps[i][:, mine])
    ubuf[0] = up_t[:, :256]
    ubuf[1] = pltpu.roll(up_t[:, 128:384], 192, 1)

    def copy_u(t, slot):
        return pltpu.make_async_remote_copy(
            src_ref=ubuf.at[lax.div(t, 8), pl.ds(pl.multiple_of(lax.rem(t, 8) * 8, 8), 8)],
            dst_ref=recv_u.at[slot],
            send_sem=send_u.at[t],
            recv_sem=got_u.at[slot],
            device_id=(t, n),
            device_id_type=MESH,
        )

    @pl.loop(1, 16)
    def _(k):
        copy_u(lax.rem(w + k, 16), w).start()

    down_t = dot_nn(backt[...], hid[...]) * NORM
    for t in range(16):
        first = 96 * t // 128 * 128
        off = 96 * t - first
        if off + 96 <= 128:
            piece = down_t[:, first : first + 128]
            piece = pltpu.roll(piece, 128 - off, 1) if off else piece
        else:
            piece = pltpu.roll(down_t[:, first : first + 256], 256 - off, 1)[:, :128]
        dbuf[t] = piece

    def copy_d(t, slot):
        return pltpu.make_async_remote_copy(
            src_ref=dbuf.at[t],
            dst_ref=recv_d.at[slot],
            send_sem=send_d.at[t],
            recv_sem=got_d.at[slot],
            device_id=(t, n),
            device_id_type=MESH,
        )

    @pl.loop(1, 16)
    def _(k):
        copy_d(lax.rem(w + k, 16), w).start()

    large(3)
    slopes(2)
    slopes(3)

    def copy_e(dn, slot):
        return pltpu.make_async_remote_copy(
            src_ref=red_u,
            dst_ref=recv_e.at[slot],
            send_sem=send_e.at[dn],
            recv_sem=got_e.at[slot],
            device_id=(e_wide, dn),
            device_id_type=MESH,
        )

    my_e_slot = lax.rem(w, 8)
    red_u[...] = ubuf[lax.div(w, 8), pl.ds(pl.multiple_of(my_e_slot * 8, 8), 8)]

    @pl.loop(1, 16)
    def _(k):
        t = lax.rem(w + k, 16)
        copy_u(t, t).wait_recv()
        red_u[...] += recv_u[t]

    @pl.loop(1, 9)
    def _(k):
        dn = lax.rem(n + k, 8)

        @pl.when(jnp.logical_or(k < 8, jnp.logical_not(e_self)))
        def _():
            copy_e(dn, my_e_slot).start()

    @pl.when(e_self)
    def _():
        recv_e[my_e_slot] = red_u[...]

    nz[1024:1280, :] = dot_nt(pc[...], weight_v[...])

    def grads(i, h):
        cols = slice(768 * h, 768 * h + 768)
        q = nz[1024 + 64 * i : 1088 + 64 * i, cols]
        q_hi = q.astype(BF16)
        q_lo = (q - q_hi.astype(F32)).astype(BF16)
        right = jnp.concatenate([q_hi, q_hi, q_lo, at_ref[:, cols]], 0)
        prods[h][...] = dot_nn(ltile[256 * i : 256 * i + 256, :], right)

    def finish(i, h):
        @pl.loop(0, 16, unroll=16)
        def _(r):
            rows = pl.ds(r * 16, 16)
            here = pl.ds(i * 256 + r * 16, 16)
            coef = ikcol[here, :]
            coef = jnp.concatenate([coef] * 3, 1)
            for s in range(2):
                cols = slice(768 * h + 384 * s, 768 * h + 384 * s + 384)
                grad = prods[h][rows, 384 * s : 384 * s + 384] - coef * nz[here, cols]
                pre_v[i, rows, cols] = (grad * slope[here, cols]).astype(BF16)

    grads(0, 0)
    for i in range(4):
        grads(i, 1)
        finish(i, 0)
        if i < 3:
            grads(i + 1, 0)
        finish(i, 1)
        out_copy(i).start()

    recv_d[w] = dbuf[w]

    @pl.loop(1, 16)
    def _(k):
        t = lax.rem(w + k, 16)
        copy_d(t, t).wait_recv()

    down = recv_d[0]
    for t in range(1, 16):
        down = down + recv_d[t]
    down_out[...] = down[:, :96]

    @pl.loop(0, 8)
    def _(k):
        @pl.when(jnp.logical_or(8 * core + k != w, lax.div(w, 2) != n))
        def _():
            copy_e(0, k).wait_recv()

    up = jnp.concatenate([recv_e[k] for k in range(8)], 0)
    up_out[...] = up[:, :192]

    @pl.loop(1, 16)
    def _(k):
        t = lax.rem(me_b + k, 16)
        copy_b(t, t, t, b_device(t)).wait_send()
        t = lax.rem(w + k, 16)
        copy_u(t, t).wait_send()
        copy_d(t, t).wait_send()

    @pl.loop(1, 9)
    def _(k):
        dn = lax.rem(n + k, 8)

        @pl.when(k < 8)
        def _():
            copy_l(dn, n).wait_send()
            copy_m(dn, n).wait_send()

        @pl.when(jnp.logical_or(k < 8, jnp.logical_not(c_self)))
        def _():
            copy_c(dn, my_c_slot).wait_send()

        @pl.when(jnp.logical_or(k < 8, jnp.logical_not(e_self)))
        def _():
            copy_e(dn, my_e_slot).wait_send()

    @pl.loop(0, 4)
    def _(i):
        out_copy(i).wait()


def main(*args):
    dma = pltpu.SemaphoreType.DMA
    v = pltpu.VMEM
    anywhere = pl.BlockSpec(memory_space=pl.ANY)
    vmem = pl.BlockSpec(memory_space=pltpu.VMEM)
    return pl.pallas_call(
        main_kernel,
        out_shape=(
            jax.ShapeDtypeStruct((4, 256, F), BF16),
            jax.ShapeDtypeStruct((64, 192), F32),
            jax.ShapeDtypeStruct((64, 96), F32),
        ),
        in_specs=[anywhere] * 10,
        out_specs=(anywhere, vmem, vmem),
        scratch_shapes=[
            v((16, 64, 128), F32),
            v((16, 64, 128), F32),
            v((16, 64, 128), F32),
            v((64, 128), F32),
            v((8, 64, 128), F32),
            v((8, 64, 128), F32),
            v((8, 64, 128), F32),
            v((64, 128), F32),
            v((8, 64, 128), F32),
            v((2, 64, 256), F32),
            v((16, 8, 256), F32),
            v((8, 256), F32),
            v((8, 8, 256), F32),
            v((16, 64, 128), F32),
            v((16, 64, 128), F32),
            v((4, 256, D), BF16),
            v((4, 256, F), BF16),
            v((F, D), BF16),
            v((256, D), BF16),
            v((256, D), BF16),
            v((256, D), BF16),
            v((256, D), BF16),
            v((256, D), BF16),
            v((128, D), BF16),
            v((128, D), BF16),
            v((1024, F), BF16),
            v((1024, F), F32),
            v((1280, F), F32),
            v((256, F // 2), F32),
            v((256, F // 2), F32),
            v((16, 128, 128), BF16),
            v((144, 512), BF16),
            v((4, 130, 16, 128), BF16),
            v((64, D), BF16),
            v((64, D), BF16),
            v((4, D), BF16),
            v((4, D), BF16),
            v((1024, 128), F32),
            v((1024, 128), F32),
            v((4, 128, 256), F32),
            v((1024, 128), F32),
            v((1024, 256), BF16),
            v((64, 1024), BF16),
            v((64, 1280), BF16),
            v((64, F), BF16),
            v((4, 8, D), F32),
            v((4, 8, D), F32),
            dma((7,)),
            dma((4,)),
            dma((4,)),
            dma((6,)),
            dma((4,)),
            dma((1,)),
            dma((1,)),
            dma((16,)),
            dma((16,)),
            dma((8,)),
            dma((8,)),
            dma((8,)),
            dma((8,)),
            dma((8,)),
            dma((8,)),
            dma((16,)),
            dma((16,)),
            dma((8,)),
            dma((8,)),
            dma((16,)),
            dma((16,)),
        ],
        compiler_params=pltpu.CompilerParams(
            collective_id=0, has_side_effects=True, vmem_limit_bytes=62 * MIB
        ),
        name="main",
    )(*args)


def place_kernel(pre, up, down, pre_out, up_out, down_out, pre_v, up_v, down_v, sem_in, sem_out):
    pieces = [
        (pre.at[i, rows], pre_v.at[i, rows], pre_out.at[i, rows])
        for i in range(4)
        for rows in (pl.ds(0, 128), pl.ds(128, 128))
    ]
    pieces += [(up, up_v, up_out), (down, down_v, down_out)]
    into = [
        pltpu.make_async_copy(src, mid, sem_in.at[k]) for k, (src, mid, _) in enumerate(pieces)
    ]
    out = [
        pltpu.make_async_copy(mid, dst, sem_out.at[k]) for k, (_, mid, dst) in enumerate(pieces)
    ]
    for copy in into:
        copy.start()
    for first, second in zip(into, out):
        first.wait()
        second.start()
    for copy in out:
        copy.wait()


def place(*arrays):
    shapes = [(a.shape, a.dtype) for a in arrays]
    anywhere = pl.BlockSpec(memory_space=pl.ANY)
    return pl.pallas_call(
        place_kernel,
        out_shape=tuple(jax.ShapeDtypeStruct(*s) for s in shapes),
        in_specs=[anywhere] * 3,
        out_specs=(anywhere,) * 3,
        scratch_shapes=[pltpu.VMEM(*s) for s in shapes]
        + [pltpu.SemaphoreType.DMA((10,)), pltpu.SemaphoreType.DMA((10,))],
        compiler_params=pltpu.CompilerParams(vmem_limit_bytes=62 * MIB),
        name="place",
    )(*arrays)


def local(
    cotangent,
    decoder_kernel,
    patch_projection_rows,
    stored_hidden_state,
    output_norm_scale,
    output_gate,
    preactivation_input,
    frozen_down_weight,
    adapter_down_rows,
    adapter_up_rows,
):
    parts = main(
        cotangent[0],
        decoder_kernel.transpose(1, 2, 0).reshape(144, 512),
        stored_hidden_state,
        preactivation_input,
        frozen_down_weight,
        adapter_down_rows.T,
        adapter_up_rows,
        patch_projection_rows,
        output_norm_scale,
        output_gate,
    )
    pre_grad, up_grad, down_grad = place(*parts)
    return pre_grad, up_grad.T, down_grad.T


def solution(mesh):
    placed = (
        P("wide", "narrow", None, None),
        P(),
        P(),
        P(None, "wide", None),
        P(),
        P(),
        P(None, "wide", "narrow"),
        P("narrow", None),
        P("narrow", None),
        P(),
    )
    return jax.shard_map(
        local,
        mesh=mesh,
        in_specs=placed,
        out_specs=(P(None, "wide", "narrow"), P("wide", None), P(("narrow", "wide"), None)),
        check_vma=False,
    )
```

```python
import jax
import jax.numpy as jnp
from jax import lax
from jax.experimental import pallas as pl
from jax.experimental.pallas import tpu as pltpu
from jax.sharding import PartitionSpec as P

MESH = pl.DeviceIdType.MESH
F32 = jnp.float32
BF16 = jnp.bfloat16
D = 3072
F = 1536
VAE_INVERSE = 1.0 / 0.3611
NORM = 1.0 / 128.0
GELU_A = 0.7978845608
MIB = 1 << 20


def dot_nt(a, b):
    return lax.dot_general(a, b, (((1,), (1,)), ((), ())), preferred_element_type=F32)


def dot_nn(a, b):
    return lax.dot_general(a, b, (((1,), (0,)), ((), ())), preferred_element_type=F32)


def dot_tn(a, b):
    return lax.dot_general(a, b, (((0,), (0,)), ((), ())), preferred_element_type=F32)


def iota(shape, axis):
    return lax.broadcasted_iota(jnp.int32, shape, axis)


def one_hot(mask):
    return mask.astype(F32).astype(BF16)


def column_taps():
    col = iota((128, 512), 1)
    return one_hot(iota((128, 512), 0) == 2 * (col & 63) - 1 + (col >> 7))


def kernel_taps():
    col = iota((16, 1024), 1)
    same = iota((16, 1024), 0) == (col & 63) >> 2
    dy = ((col >> 1) & 1) + 2 - (col >> 8)
    dx = (col & 1) + 2 - ((col >> 6) & 3)
    return jnp.concatenate(
        [one_hot(same & (dy == t // 3) & (dx == t % 3)) for t in range(9)], 0
    )


def main_kernel(
    cot,
    taps_in,
    stored,
    pre,
    weight,
    a_in,
    u_in,
    p_in,
    scale_in,
    gate_in,
    pre_out,
    up_out,
    down_out,
    own,
    recv_a,
    recv_b,
    red,
    recv_c,
    low_part,
    recv_l,
    red_l,
    recv_m,
    ubuf,
    recv_u,
    red_u,
    recv_e,
    dbuf,
    recv_d,
    stored_v,
    pre_v,
    weight_v,
    z0,
    z1,
    z2,
    z3,
    pc,
    xw0,
    xw1,
    hid,
    slope,
    nz,
    prod0,
    prod1,
    cot_v,
    taps_v,
    g_ref,
    u_ref,
    p_ref,
    scale_ref,
    gate_ref,
    meanb,
    invb,
    vbt,
    ikcol,
    ltile,
    backt,
    klt,
    at_ref,
    gate_v,
    scale_v,
    sem_local,
    sem_pre,
    sem_stored,
    sem_weight,
    sem_out,
    send_a,
    got_a,
    send_b,
    got_b,
    send_c,
    got_c,
    send_l,
    got_l,
    send_m,
    got_m,
    send_u,
    got_u,
    send_e,
    got_e,
    send_d,
    got_d,
):
    zps = (z0, z1, z2, z3)
    xws = (xw0, xw1)
    prods = (prod0, prod1)
    w = lax.axis_index("wide")
    n = lax.axis_index("narrow")
    img = lax.div(w, 4)
    grp = lax.rem(w, 4)
    core = lax.rem(w, 2)
    me_b = lax.div(grp, 2) * 8 + n
    c_wide = 4 * lax.div(n, 2) + grp
    e_wide = 2 * n + lax.div(w, 8)
    c_self = c_wide == w
    e_self = e_wide == w

    small = [
        pltpu.make_async_copy(src, dst, sem_local.at[k])
        for k, (src, dst) in enumerate(
            [
                (cot, cot_v),
                (taps_in, taps_v),
                (a_in, at_ref),
                (gate_in, gate_ref),
                (scale_in, scale_ref),
                (p_in, p_ref),
                (u_in, u_ref),
            ]
        )
    ]
    for copy in small:
        copy.start()

    def pre_copy(i):
        return pltpu.make_async_copy(pre.at[i], pre_v.at[i], sem_pre.at[i])

    def stored_copy(i):
        return pltpu.make_async_copy(stored.at[i], stored_v.at[i], sem_stored.at[i])

    def weight_copy(j):
        rows = pl.ds(pl.multiple_of(j * 256, 256), 256)
        return pltpu.make_async_copy(weight.at[rows], weight_v.at[rows], sem_weight.at[j])

    def out_copy(i):
        return pltpu.make_async_copy(pre_v.at[i], pre_out.at[i], sem_out.at[i])

    stored_copy(0).start()

    @pl.loop(0, 6)
    def _(j):
        weight_copy(j).start()

    stored_copy(1).start()

    @pl.loop(0, 4)
    def _(i):
        pre_copy(i).start()

    stored_copy(2).start()
    stored_copy(3).start()

    barrier = pltpu.get_barrier_semaphore()

    def greet(dw, dn):
        pl.semaphore_signal(barrier, inc=1, device_id=(dw, dn), device_id_type=MESH)

    def b_device(t):
        return 4 * img + 2 * lax.div(t, 8) + core, lax.rem(t, 8)

    @pl.loop(1, 16)
    def _(k):
        greet(*b_device(lax.rem(me_b + k, 16)))
        greet(lax.rem(w + k, 16), n)

    @pl.loop(0, 8)
    def _(k):
        cw, cn = 4 * lax.div(k, 2) + grp, 2 * img + lax.rem(k, 2)

        @pl.when(jnp.logical_or(cw != w, cn != n))
        def _():
            greet(cw, cn)

        ew, en = 8 * core + k, lax.div(w, 2)

        @pl.when(jnp.logical_or(ew != w, en != n))
        def _():
            greet(ew, en)

    zero = jnp.zeros((16, 128), BF16)
    for tap in range(4):
        g_ref[tap, 0] = zero
        g_ref[tap, 129] = zero
    columns = column_taps()
    routes = kernel_taps()
    pick = one_hot(iota((16, 512), 1) - grp * 128 - n * 16 == iota((16, 512), 0))
    small[0].wait()
    small[1].wait()
    mine = dot_nn(dot_nt(pick, taps_v[...]).astype(BF16), routes)
    mine = jnp.concatenate([mine[:, 64 * t : 64 * t + 64] for t in range(16)], 0)
    for r in range(4):
        rows = jnp.swapaxes(cot_v[:, 32 * r : 32 * r + 32, :], 0, 1).reshape(512, 128)
        moved = dot_nn(rows, columns).astype(BF16)
        for tap in range(4):
            g_ref[tap, 1 + 32 * r : 33 + 32 * r] = moved[:, 128 * tap : 128 * tap + 128].reshape(
                32, 16, 128
            )

    weights = jnp.transpose(mine).astype(BF16)
    left_half = iota((16, 128), 1) < 64

    def conv(side, dst):
        @pl.loop(0, 4)
        def _(quarter):
            for z in range(2):
                for half in range(2):
                    row = 32 * quarter + 16 * z + 8 * side + 4 * half
                    window = [
                        jnp.where(left_half, g_ref[tx, row + ty], g_ref[tx, row + 2 + ty])
                        for ty in range(4)
                        for tx in range(4)
                    ]
                    dst[8 * z + 2 * quarter + half] = dot_nn(
                        weights, jnp.concatenate(window, 0)
                    )

    conv(1 - core, dbuf)
    conv(core, own)
    pl.semaphore_wait(barrier, 46 - c_self.astype(jnp.int32) - e_self.astype(jnp.int32))

    copy_a = pltpu.make_async_remote_copy(
        src_ref=dbuf,
        dst_ref=recv_a,
        send_sem=send_a.at[0],
        recv_sem=got_a.at[0],
        device_id=(w + 1 - 2 * core, n),
        device_id_type=MESH,
    )
    copy_a.start()
    for copy in small[2:]:
        copy.wait()

    def all_of(ref, count, send, got):
        some = ref.at[pl.ds(0, count)]
        return pltpu.make_async_remote_copy(
            src_ref=some,
            dst_ref=some,
            send_sem=send.at[0],
            recv_sem=got.at[0],
            device_id=(w, lax.rem(n + 1, 8)),
            device_id_type=MESH,
        )

    def sum_of(ref, count):
        acc = ref[0]
        for k in range(1, count):
            acc = acc + ref[k]
        return acc

    def copy_b(src, slot, t, dev):
        return pltpu.make_async_remote_copy(
            src_ref=own.at[src],
            dst_ref=recv_b.at[slot],
            send_sem=send_b.at[0],
            recv_sem=got_b.at[0],
            device_id=dev,
            device_id_type=MESH,
        )

    def start_b():
        copy_a.wait()

        @pl.loop(1, 17)
        def _(k):
            t = lax.rem(me_b + k, 16)
            own[t] = own[t] + recv_a[t]

            @pl.when(k < 16)
            def _():
                copy_b(t, me_b, t, b_device(t)).start()

    gates = gate_ref[...].astype(F32)
    scales = 1.0 + scale_ref[...].astype(F32)
    for i in range(4):
        gate_v[i] = jnp.broadcast_to(gates[i : i + 1], (8, D))
        scale_v[i] = jnp.broadcast_to(scales[i : i + 1], (8, D))

    def stats(i):
        @pl.loop(0, 16, unroll=16)
        def _(r):
            acc = jnp.zeros((16, 128), F32)
            for s in range(24):
                cols = slice(128 * s, 128 * s + 128)
                acc += stored_v[i, pl.ds(r * 16, 16), cols].astype(F32)
            meanb[pl.ds(i * 256 + r * 16, 16), :] = acc

        tokens = slice(256 * i, 256 * i + 256)
        mean = jnp.sum(meanb[tokens, :], axis=1, keepdims=True) * (1.0 / D)
        meanb[tokens, :] = jnp.broadcast_to(mean, (256, 128))

        @pl.loop(0, 16, unroll=16)
        def _(r):
            here = pl.ds(i * 256 + r * 16, 16)
            mean = meanb[here, :]
            acc = jnp.zeros((16, 128), F32)
            for s in range(24):
                cols = slice(128 * s, 128 * s + 128)
                x = stored_v[i, pl.ds(r * 16, 16), cols].astype(F32) - mean
                zps[i][pl.ds(r * 16, 16), cols] = (x * gate_v[i, 0:1, cols]).astype(BF16)
                acc += x * x
            invb[here, :] = acc

        var = jnp.sum(invb[tokens, :], axis=1, keepdims=True) * (1.0 / D)
        invb[tokens, :] = jnp.broadcast_to(1.0 / jnp.sqrt(var + 1e-06), (256, 128))

    def prep(i):
        def total(s, acc):
            cols = pl.ds(128 * s, 128)
            return acc + p_ref[:, cols].astype(F32) * scale_v[i, 0:1, cols]

        acc = lax.fori_loop(0, 24, total, jnp.zeros((64, 128), F32), unroll=24)
        mean = jnp.broadcast_to(jnp.sum(acc, axis=1, keepdims=True) * (1.0 / D), (64, 128))

        def fill(s, acc):
            cols = pl.ds(128 * s, 128)
            gate = gate_v[i, 0:1, cols]
            x = p_ref[:, cols].astype(F32) * scale_v[i, 0:1, cols] - mean
            pc[64 * i : 64 * i + 64, cols] = (x * gate).astype(BF16)
            both = jnp.concatenate([x, u_ref[:, cols].astype(F32) * gate], 0).astype(BF16)
            xws[i % 2][:, cols] = both
            return acc + both.astype(F32)

        acc = lax.fori_loop(0, 24, fill, jnp.zeros((128, 128), F32), unroll=24)
        return jnp.sum(acc, axis=1, keepdims=True)

    def large(i):
        nz[256 * i : 256 * i + 256, :] = dot_nt(zps[i][...], weight_v[...])

    def small_products(i, sums):
        tokens = slice(256 * i, 256 * i + 256)
        mean_row = jnp.transpose(meanb[tokens, :])[:1, :]
        vbt[i] = dot_nt(xws[i % 2][...], stored_v[i]) - sums * mean_row

    def gelu(i):
        @pl.loop(0, 16, unroll=16)
        def _(r):
            rows = pl.ds(r * 16, 16)
            here = pl.ds(i * 256 + r * 16, 16)
            for s in range(3):
                cols = slice(512 * s, 512 * s + 512)
                m = pre_v[i, rows, cols].astype(F32)
                h = 0.5 + 0.5 * jnp.tanh(m * (GELU_A + (GELU_A * 0.044715) * (m * m)))
                hid[here, cols] = (m * h).astype(BF16)

    def slopes(i):
        @pl.loop(0, 16, unroll=16)
        def _(r):
            rows = pl.ds(r * 16, 16)
            here = pl.ds(i * 256 + r * 16, 16)
            for s in range(3):
                cols = slice(512 * s, 512 * s + 512)
                m = pre_v[i, rows, cols].astype(F32)
                sq = m * m
                h = 0.5 + 0.5 * jnp.tanh(m * (GELU_A + (GELU_A * 0.044715) * sq))
                slope[here, cols] = h + (2.0 * m) * h * (1.0 - h) * (
                    GELU_A + (GELU_A * 0.134145) * sq
                )

    stored_copy(0).wait()
    sums = prep(0)
    stats(0)
    start_b()

    def copy_l(t, slot):
        return pltpu.make_async_remote_copy(
            src_ref=low_part.at[t],
            dst_ref=recv_l.at[slot],
            send_sem=send_l.at[0],
            recv_sem=got_l.at[0],
            device_id=(w, t),
            device_id_type=MESH,
        )

    @pl.loop(0, 6)
    def _(j):
        weight_copy(j).wait()

    stored_copy(1).wait()
    for i in range(4):
        pre_copy(i).wait()
    large(0)
    small_products(0, sums)
    stats(1)
    sums = prep(1)
    for i in range(4):
        gelu(i)
    for i in range(4):
        lt = dot_nt(at_ref[...], hid[256 * i : 256 * i + 256, :])
        low_part[2 * i] = lt[:, :128]
        low_part[2 * i + 1] = lt[:, 128:]

    @pl.loop(1, 8)
    def _(k):
        copy_l(lax.rem(n + k, 8), n).start()

    stored_copy(2).wait()
    large(1)
    small_products(1, sums)
    stats(2)
    sums = prep(2)

    def copy_c(dn, slot):
        return pltpu.make_async_remote_copy(
            src_ref=red,
            dst_ref=recv_c.at[slot],
            send_sem=send_c.at[0],
            recv_sem=got_c.at[0],
            device_id=(c_wide, dn),
            device_id_type=MESH,
        )

    my_c_slot = 2 * img + lax.rem(n, 2)
    recv_b[me_b] = own[me_b]
    all_of(recv_b, 15, send_b, got_b).wait_recv()
    red[...] = sum_of(recv_b, 16)

    @pl.loop(1, 9)
    def _(k):
        dn = lax.rem(n + k, 8)

        @pl.when(jnp.logical_or(k < 8, jnp.logical_not(c_self)))
        def _():
            copy_c(dn, my_c_slot).start()

    @pl.when(c_self)
    def _():
        recv_c[my_c_slot] = red[...]

    def copy_m(t, slot):
        return pltpu.make_async_remote_copy(
            src_ref=red_l,
            dst_ref=recv_m.at[slot],
            send_sem=send_m.at[0],
            recv_sem=got_m.at[0],
            device_id=(w, t),
            device_id_type=MESH,
        )

    recv_l[n] = low_part[n]
    all_of(recv_l, 7, send_l, got_l).wait_recv()
    red_l[...] = sum_of(recv_l, 8)
    recv_m[n] = red_l[...]

    @pl.loop(1, 8)
    def _(k):
        copy_m(lax.rem(n + k, 8), n).start()

    stored_copy(3).wait()
    large(2)
    small_products(2, sums)
    stats(3)
    sums = prep(3)
    slopes(0)
    slopes(1)
    small_products(3, sums)
    put = dot_nt(u_ref[...], pc[...])

    @pl.when(c_self)
    def _():
        all_of(recv_c, 7, send_c, got_c).wait_recv()

    @pl.when(jnp.logical_not(c_self))
    def _():
        all_of(recv_c, 8, send_c, got_c).wait_recv()

    all_of(recv_m, 7, send_m, got_m).wait_recv()

    t1 = []
    for i in range(4):
        tok = slice(256 * i, 256 * i + 256)
        lat = jnp.concatenate([recv_c[2 * i], recv_c[2 * i + 1]], 1)
        pat = (lat * VAE_INVERSE).astype(BF16)
        pf = pat.astype(F32)
        inv = jnp.transpose(invb[tok, :])[:1, :]
        vb = vbt[i]
        k_row = inv * inv * (jnp.sum(pf * vb[:64], axis=0, keepdims=True) * (1.0 / D))
        pu = put[:, 64 * i : 64 * i + 64]
        pu_hi = pu.astype(BF16)
        pu_lo = (pu - pu_hi.astype(F32)).astype(BF16)
        back = (inv * (dot_nn(pu_hi, pat) + dot_nn(pu_lo, pat) - k_row * vb[64:])).astype(BF16)
        ip = inv * pf
        ip_hi = ip.astype(BF16)
        ip_lo = (ip - ip_hi.astype(F32)).astype(BF16)
        backt[:, tok] = back
        stack = jnp.concatenate([ip_hi, ip_lo, ip_hi, back], 0)
        ltile[tok, :] = jnp.transpose(stack.astype(F32)).astype(BF16)
        ik = inv * k_row
        ikcol[tok, :] = jnp.transpose(jnp.broadcast_to(ik, (128, 256)))
        low = (jnp.concatenate([recv_m[2 * i], recv_m[2 * i + 1]], 1) * NORM).astype(BF16)
        klt[:, tok] = (-ik * low.astype(F32)).astype(BF16)
        t1.append(dot_nt(low, ip_hi) + dot_nt(low, ip_lo))
    klt[:, 1024:1280] = jnp.concatenate(t1, 1).astype(BF16)

    mine = pl.ds(pl.multiple_of(n * 384, 128), 384)
    up_t = dot_nn(klt[:, 1024:1280], pc[:, mine])
    for i in range(4):
        up_t += dot_nn(klt[:, 256 * i : 256 * i + 256], zps[i][:, mine])
    ubuf[0] = up_t[:, :256]
    ubuf[1] = pltpu.roll(up_t[:, 128:384], 192, 1)

    def copy_u(t, slot):
        return pltpu.make_async_remote_copy(
            src_ref=ubuf.at[lax.div(t, 8), pl.ds(pl.multiple_of(lax.rem(t, 8) * 8, 8), 8)],
            dst_ref=recv_u.at[slot],
            send_sem=send_u.at[0],
            recv_sem=got_u.at[0],
            device_id=(t, n),
            device_id_type=MESH,
        )

    @pl.loop(1, 16)
    def _(k):
        copy_u(lax.rem(w + k, 16), w).start()

    down_t = dot_nn(backt[...], hid[...]) * NORM
    for t in range(16):
        first = 96 * t // 128 * 128
        off = 96 * t - first
        if off + 96 <= 128:
            piece = down_t[:, first : first + 128]
            piece = pltpu.roll(piece, 128 - off, 1) if off else piece
        else:
            piece = pltpu.roll(down_t[:, first : first + 256], 256 - off, 1)[:, :128]
        dbuf[t] = piece

    def copy_d(t, slot):
        return pltpu.make_async_remote_copy(
            src_ref=dbuf.at[t],
            dst_ref=recv_d.at[slot],
            send_sem=send_d.at[0],
            recv_sem=got_d.at[0],
            device_id=(t, n),
            device_id_type=MESH,
        )

    @pl.loop(1, 16)
    def _(k):
        copy_d(lax.rem(w + k, 16), w).start()

    large(3)
    slopes(2)
    slopes(3)

    def copy_e(dn, slot):
        return pltpu.make_async_remote_copy(
            src_ref=red_u,
            dst_ref=recv_e.at[slot],
            send_sem=send_e.at[0],
            recv_sem=got_e.at[0],
            device_id=(e_wide, dn),
            device_id_type=MESH,
        )

    my_e_slot = lax.rem(w, 8)
    recv_u[w] = ubuf[lax.div(w, 8), pl.ds(pl.multiple_of(my_e_slot * 8, 8), 8)]
    all_of(recv_u, 15, send_u, got_u).wait_recv()
    red_u[...] = sum_of(recv_u, 16)

    @pl.loop(1, 9)
    def _(k):
        dn = lax.rem(n + k, 8)

        @pl.when(jnp.logical_or(k < 8, jnp.logical_not(e_self)))
        def _():
            copy_e(dn, my_e_slot).start()

    @pl.when(e_self)
    def _():
        recv_e[my_e_slot] = red_u[...]

    nz[1024:1280, :] = dot_nt(pc[...], weight_v[...])

    def grads(i, h):
        cols = slice(768 * h, 768 * h + 768)
        q = nz[1024 + 64 * i : 1088 + 64 * i, cols]
        q_hi = q.astype(BF16)
        q_lo = (q - q_hi.astype(F32)).astype(BF16)
        right = jnp.concatenate([q_hi, q_hi, q_lo, at_ref[:, cols]], 0)
        prods[h][...] = dot_nn(ltile[256 * i : 256 * i + 256, :], right)

    def finish(i, h):
        @pl.loop(0, 16, unroll=16)
        def _(r):
            rows = pl.ds(r * 16, 16)
            here = pl.ds(i * 256 + r * 16, 16)
            coef = ikcol[here, :]
            coef = jnp.concatenate([coef] * 3, 1)
            for s in range(2):
                cols = slice(768 * h + 384 * s, 768 * h + 384 * s + 384)
                grad = prods[h][rows, 384 * s : 384 * s + 384] - coef * nz[here, cols]
                pre_v[i, rows, cols] = (grad * slope[here, cols]).astype(BF16)

    grads(0, 0)
    for i in range(4):
        grads(i, 1)
        finish(i, 0)
        if i < 3:
            grads(i + 1, 0)
        finish(i, 1)
        out_copy(i).start()

    recv_d[w] = dbuf[w]
    all_of(recv_d, 15, send_d, got_d).wait_recv()
    down_out[...] = sum_of(recv_d, 16)[:, :96]

    @pl.when(e_self)
    def _():
        all_of(recv_e, 7, send_e, got_e).wait_recv()

    @pl.when(jnp.logical_not(e_self))
    def _():
        all_of(recv_e, 8, send_e, got_e).wait_recv()

    up = jnp.concatenate([recv_e[k] for k in range(8)], 0)
    up_out[...] = up[:, :192]

    all_of(recv_b, 15, send_b, got_b).wait_send()
    all_of(recv_l, 7, send_l, got_l).wait_send()
    all_of(recv_m, 7, send_m, got_m).wait_send()
    all_of(recv_u, 15, send_u, got_u).wait_send()
    all_of(recv_d, 15, send_d, got_d).wait_send()

    @pl.when(c_self)
    def _():
        all_of(recv_c, 7, send_c, got_c).wait_send()

    @pl.when(jnp.logical_not(c_self))
    def _():
        all_of(recv_c, 8, send_c, got_c).wait_send()

    @pl.when(e_self)
    def _():
        all_of(recv_e, 7, send_e, got_e).wait_send()

    @pl.when(jnp.logical_not(e_self))
    def _():
        all_of(recv_e, 8, send_e, got_e).wait_send()

    @pl.loop(0, 4)
    def _(i):
        out_copy(i).wait()


def main(*args):
    dma = pltpu.SemaphoreType.DMA
    v = pltpu.VMEM
    anywhere = pl.BlockSpec(memory_space=pl.ANY)
    vmem = pl.BlockSpec(memory_space=pltpu.VMEM)
    return pl.pallas_call(
        main_kernel,
        out_shape=(
            jax.ShapeDtypeStruct((4, 256, F), BF16),
            jax.ShapeDtypeStruct((64, 192), F32),
            jax.ShapeDtypeStruct((64, 96), F32),
        ),
        in_specs=[anywhere] * 10,
        out_specs=(anywhere, vmem, vmem),
        scratch_shapes=[
            v((16, 64, 128), F32),
            v((16, 64, 128), F32),
            v((16, 64, 128), F32),
            v((64, 128), F32),
            v((8, 64, 128), F32),
            v((8, 64, 128), F32),
            v((8, 64, 128), F32),
            v((64, 128), F32),
            v((8, 64, 128), F32),
            v((2, 64, 256), F32),
            v((16, 8, 256), F32),
            v((8, 256), F32),
            v((8, 8, 256), F32),
            v((16, 64, 128), F32),
            v((16, 64, 128), F32),
            v((4, 256, D), BF16),
            v((4, 256, F), BF16),
            v((F, D), BF16),
            v((256, D), BF16),
            v((256, D), BF16),
            v((256, D), BF16),
            v((256, D), BF16),
            v((256, D), BF16),
            v((128, D), BF16),
            v((128, D), BF16),
            v((1024, F), BF16),
            v((1024, F), F32),
            v((1280, F), F32),
            v((256, F // 2), F32),
            v((256, F // 2), F32),
            v((16, 128, 128), BF16),
            v((144, 512), BF16),
            v((4, 130, 16, 128), BF16),
            v((64, D), BF16),
            v((64, D), BF16),
            v((4, D), BF16),
            v((4, D), BF16),
            v((1024, 128), F32),
            v((1024, 128), F32),
            v((4, 128, 256), F32),
            v((1024, 128), F32),
            v((1024, 256), BF16),
            v((64, 1024), BF16),
            v((64, 1280), BF16),
            v((64, F), BF16),
            v((4, 8, D), F32),
            v((4, 8, D), F32),
            dma((7,)),
            dma((4,)),
            dma((4,)),
            dma((6,)),
            dma((4,)),
            dma((1,)),
            dma((1,)),
            dma((1,)),
            dma((1,)),
            dma((1,)),
            dma((1,)),
            dma((1,)),
            dma((1,)),
            dma((1,)),
            dma((1,)),
            dma((1,)),
            dma((1,)),
            dma((1,)),
            dma((1,)),
            dma((1,)),
            dma((1,)),
        ],
        compiler_params=pltpu.CompilerParams(
            collective_id=0, has_side_effects=True, vmem_limit_bytes=62 * MIB
        ),
        name="main",
    )(*args)


def place_kernel(pre, up, down, pre_out, up_out, down_out, pre_v, up_v, down_v, sem_in, sem_out):
    pieces = [
        (pre.at[i, rows], pre_v.at[i, rows], pre_out.at[i, rows])
        for i in range(4)
        for rows in (pl.ds(0, 128), pl.ds(128, 128))
    ]
    pieces += [(up, up_v, up_out), (down, down_v, down_out)]
    into = [
        pltpu.make_async_copy(src, mid, sem_in.at[k]) for k, (src, mid, _) in enumerate(pieces)
    ]
    out = [
        pltpu.make_async_copy(mid, dst, sem_out.at[k]) for k, (_, mid, dst) in enumerate(pieces)
    ]
    for copy in into:
        copy.start()
    for first, second in zip(into, out):
        first.wait()
        second.start()
    for copy in out:
        copy.wait()


def place(*arrays):
    shapes = [(a.shape, a.dtype) for a in arrays]
    anywhere = pl.BlockSpec(memory_space=pl.ANY)
    return pl.pallas_call(
        place_kernel,
        out_shape=tuple(jax.ShapeDtypeStruct(*s) for s in shapes),
        in_specs=[anywhere] * 3,
        out_specs=(anywhere,) * 3,
        scratch_shapes=[pltpu.VMEM(*s) for s in shapes]
        + [pltpu.SemaphoreType.DMA((10,)), pltpu.SemaphoreType.DMA((10,))],
        compiler_params=pltpu.CompilerParams(vmem_limit_bytes=62 * MIB),
        name="place",
    )(*arrays)


def local(
    cotangent,
    decoder_kernel,
    patch_projection_rows,
    stored_hidden_state,
    output_norm_scale,
    output_gate,
    preactivation_input,
    frozen_down_weight,
    adapter_down_rows,
    adapter_up_rows,
):
    parts = main(
        cotangent[0],
        decoder_kernel.transpose(1, 2, 0).reshape(144, 512),
        stored_hidden_state,
        preactivation_input,
        frozen_down_weight,
        adapter_down_rows.T,
        adapter_up_rows,
        patch_projection_rows,
        output_norm_scale,
        output_gate,
    )
    pre_grad, up_grad, down_grad = place(*parts)
    return pre_grad, up_grad.T, down_grad.T


def solution(mesh):
    placed = (
        P("wide", "narrow", None, None),
        P(),
        P(),
        P(None, "wide", None),
        P(),
        P(),
        P(None, "wide", "narrow"),
        P("narrow", None),
        P("narrow", None),
        P(),
    )
    return jax.shard_map(
        local,
        mesh=mesh,
        in_specs=placed,
        out_specs=(P(None, "wide", "narrow"), P("wide", None), P(("narrow", "wide"), None)),
        check_vma=False,
    )
```

```python
import jax
import jax.numpy as jnp
from jax import lax
from jax.experimental import pallas as pl
from jax.experimental.pallas import tpu as pltpu
from jax.sharding import PartitionSpec as P

MESH = pl.DeviceIdType.MESH
F32 = jnp.float32
BF16 = jnp.bfloat16
D = 3072
F = 1536
VAE_INVERSE = 1.0 / 0.3611
NORM = 1.0 / 128.0
GELU_A = 0.7978845608
MIB = 1 << 20


def dot_nt(a, b):
    return lax.dot_general(a, b, (((1,), (1,)), ((), ())), preferred_element_type=F32)


def dot_nn(a, b):
    return lax.dot_general(a, b, (((1,), (0,)), ((), ())), preferred_element_type=F32)


def dot_tn(a, b):
    return lax.dot_general(a, b, (((0,), (0,)), ((), ())), preferred_element_type=F32)


def iota(shape, axis):
    return lax.broadcasted_iota(jnp.int32, shape, axis)


def one_hot(mask):
    return mask.astype(F32).astype(BF16)


def column_taps():
    col = iota((128, 512), 1)
    return one_hot(iota((128, 512), 0) == 2 * (col & 63) - 1 + (col >> 7))


def kernel_taps():
    col = iota((16, 1024), 1)
    same = iota((16, 1024), 0) == (col & 63) >> 2
    dy = ((col >> 1) & 1) + 2 - (col >> 8)
    dx = (col & 1) + 2 - ((col >> 6) & 3)
    return jnp.concatenate(
        [one_hot(same & (dy == t // 3) & (dx == t % 3)) for t in range(9)], 0
    )


def main_kernel(
    cot,
    taps_in,
    stored,
    pre,
    weight,
    a_in,
    u_in,
    p_in,
    scale_in,
    gate_in,
    pre_out,
    up_out,
    down_out,
    own,
    recv_a,
    recv_b,
    red,
    recv_c,
    low_part,
    recv_l,
    red_l,
    recv_m,
    ubuf,
    recv_u,
    red_u,
    recv_e,
    dbuf,
    recv_d,
    stored_v,
    pre_v,
    weight_v,
    z0,
    z1,
    z2,
    z3,
    pc,
    xw0,
    xw1,
    hid,
    slope,
    nz,
    prod0,
    prod1,
    cot_v,
    taps_v,
    g_ref,
    u_ref,
    p_ref,
    scale_ref,
    gate_ref,
    meanb,
    invb,
    vbt,
    ikcol,
    ltile,
    backt,
    klt,
    at_ref,
    gate_v,
    scale_v,
    sem_local,
    sem_pre,
    sem_stored,
    sem_weight,
    sem_out,
    send_a,
    got_a,
    send_b,
    got_b,
    send_c,
    got_c,
    send_l,
    got_l,
    send_m,
    got_m,
    send_u,
    got_u,
    send_e,
    got_e,
    send_d,
    got_d,
):
    zps = (z0, z1, z2, z3)
    xws = (xw0, xw1)
    prods = (prod0, prod1)
    w = lax.axis_index("wide")
    n = lax.axis_index("narrow")
    img = lax.div(w, 4)
    grp = lax.rem(w, 4)
    core = lax.rem(w, 2)
    me_b = lax.div(grp, 2) * 8 + n
    c_wide = 4 * lax.div(n, 2) + grp
    e_wide = 2 * n + lax.div(w, 8)
    c_self = c_wide == w
    e_self = e_wide == w

    small = [
        pltpu.make_async_copy(src, dst, sem_local.at[k])
        for k, (src, dst) in enumerate(
            [
                (cot, cot_v),
                (taps_in, taps_v),
                (a_in, at_ref),
                (gate_in, gate_ref),
                (scale_in, scale_ref),
                (p_in, p_ref),
                (u_in, u_ref),
            ]
        )
    ]
    for copy in small:
        copy.start()

    def pre_copy(i):
        return pltpu.make_async_copy(pre.at[i], pre_v.at[i], sem_pre.at[i])

    def stored_copy(i):
        return pltpu.make_async_copy(stored.at[i], stored_v.at[i], sem_stored.at[i])

    def weight_copy(j):
        rows = pl.ds(pl.multiple_of(j * 256, 256), 256)
        return pltpu.make_async_copy(weight.at[rows], weight_v.at[rows], sem_weight.at[j])

    def out_copy(i):
        return pltpu.make_async_copy(pre_v.at[i], pre_out.at[i], sem_out.at[i])

    stored_copy(0).start()

    @pl.loop(0, 6)
    def _(j):
        weight_copy(j).start()

    stored_copy(1).start()

    @pl.loop(0, 4)
    def _(i):
        pre_copy(i).start()

    stored_copy(2).start()
    stored_copy(3).start()

    barrier = pltpu.get_barrier_semaphore()

    def greet(dw, dn):
        pl.semaphore_signal(barrier, inc=1, device_id=(dw, dn), device_id_type=MESH)

    def b_device(t):
        return 4 * img + 2 * lax.div(t, 8) + core, lax.rem(t, 8)

    @pl.loop(1, 16)
    def _(k):
        greet(*b_device(lax.rem(me_b + k, 16)))
        greet(lax.rem(w + k, 16), n)

    @pl.loop(0, 8)
    def _(k):
        cw, cn = 4 * lax.div(k, 2) + grp, 2 * img + lax.rem(k, 2)

        @pl.when(jnp.logical_or(cw != w, cn != n))
        def _():
            greet(cw, cn)

        ew, en = 8 * core + k, lax.div(w, 2)

        @pl.when(jnp.logical_or(ew != w, en != n))
        def _():
            greet(ew, en)

    zero = jnp.zeros((16, 128), BF16)
    for tap in range(4):
        g_ref[tap, 0] = zero
        g_ref[tap, 129] = zero
    columns = column_taps()
    routes = kernel_taps()
    pick = one_hot(iota((16, 512), 1) - grp * 128 - n * 16 == iota((16, 512), 0))
    small[0].wait()
    small[1].wait()
    mine = dot_nn(dot_nt(pick, taps_v[...]).astype(BF16), routes)
    mine = jnp.concatenate([mine[:, 64 * t : 64 * t + 64] for t in range(16)], 0)
    for r in range(4):
        rows = jnp.swapaxes(cot_v[:, 32 * r : 32 * r + 32, :], 0, 1).reshape(512, 128)
        moved = dot_nn(rows, columns).astype(BF16)
        for tap in range(4):
            g_ref[tap, 1 + 32 * r : 33 + 32 * r] = moved[:, 128 * tap : 128 * tap + 128].reshape(
                32, 16, 128
            )

    weights = jnp.transpose(mine).astype(BF16)
    left_half = iota((16, 128), 1) < 64

    def conv(side, dst):
        @pl.loop(0, 4)
        def _(quarter):
            for z in range(2):
                for half in range(2):
                    row = 32 * quarter + 16 * z + 8 * side + 4 * half
                    window = [
                        jnp.where(left_half, g_ref[tx, row + ty], g_ref[tx, row + 2 + ty])
                        for ty in range(4)
                        for tx in range(4)
                    ]
                    dst[8 * z + 2 * quarter + half] = dot_nn(
                        weights, jnp.concatenate(window, 0)
                    )

    conv(1 - core, dbuf)
    conv(core, own)
    pl.semaphore_wait(barrier, 46 - c_self.astype(jnp.int32) - e_self.astype(jnp.int32))

    copy_a = pltpu.make_async_remote_copy(
        src_ref=dbuf,
        dst_ref=recv_a,
        send_sem=send_a.at[0],
        recv_sem=got_a.at[0],
        device_id=(w + 1 - 2 * core, n),
        device_id_type=MESH,
    )
    copy_a.start()
    for copy in small[2:]:
        copy.wait()

    def all_of(ref, count, send, got):
        some = ref.at[pl.ds(0, count)]
        return pltpu.make_async_remote_copy(
            src_ref=some,
            dst_ref=some,
            send_sem=send.at[0],
            recv_sem=got.at[0],
            device_id=(w, lax.rem(n + 1, 8)),
            device_id_type=MESH,
        )

    def sum_of(ref, count):
        acc = ref[0]
        for k in range(1, count):
            acc = acc + ref[k]
        return acc

    def copy_b(src, slot, t, dev):
        return pltpu.make_async_remote_copy(
            src_ref=own.at[src],
            dst_ref=recv_b.at[slot],
            send_sem=send_b.at[0],
            recv_sem=got_b.at[0],
            device_id=dev,
            device_id_type=MESH,
        )

    def start_b():
        copy_a.wait()

        @pl.loop(1, 17)
        def _(k):
            t = lax.rem(me_b + k, 16)
            own[t] = own[t] + recv_a[t]

            @pl.when(k < 16)
            def _():
                copy_b(t, me_b, t, b_device(t)).start()

    gates = gate_ref[...].astype(F32)
    scales = 1.0 + scale_ref[...].astype(F32)
    for i in range(4):
        gate_v[i] = jnp.broadcast_to(gates[i : i + 1], (8, D))
        scale_v[i] = jnp.broadcast_to(scales[i : i + 1], (8, D))

    def stats(i):
        @pl.loop(0, 16, unroll=16)
        def _(r):
            acc = jnp.zeros((16, 128), F32)
            for s in range(24):
                cols = slice(128 * s, 128 * s + 128)
                acc += stored_v[i, pl.ds(r * 16, 16), cols].astype(F32)
            meanb[pl.ds(i * 256 + r * 16, 16), :] = acc

        tokens = slice(256 * i, 256 * i + 256)
        mean = jnp.sum(meanb[tokens, :], axis=1, keepdims=True) * (1.0 / D)
        meanb[tokens, :] = jnp.broadcast_to(mean, (256, 128))

        @pl.loop(0, 16, unroll=16)
        def _(r):
            here = pl.ds(i * 256 + r * 16, 16)
            mean = meanb[here, :]
            acc = jnp.zeros((16, 128), F32)
            for s in range(24):
                cols = slice(128 * s, 128 * s + 128)
                x = stored_v[i, pl.ds(r * 16, 16), cols].astype(F32) - mean
                zps[i][pl.ds(r * 16, 16), cols] = (x * gate_v[i, 0:1, cols]).astype(BF16)
                acc += x * x
            invb[here, :] = acc

        var = jnp.sum(invb[tokens, :], axis=1, keepdims=True) * (1.0 / D)
        invb[tokens, :] = jnp.broadcast_to(1.0 / jnp.sqrt(var + 1e-06), (256, 128))

    def prep(i):
        def total(s, acc):
            cols = pl.ds(128 * s, 128)
            return acc + p_ref[:, cols].astype(F32) * scale_v[i, 0:1, cols]

        acc = lax.fori_loop(0, 24, total, jnp.zeros((64, 128), F32), unroll=24)
        mean = jnp.broadcast_to(jnp.sum(acc, axis=1, keepdims=True) * (1.0 / D), (64, 128))

        def fill(s, acc):
            cols = pl.ds(128 * s, 128)
            gate = gate_v[i, 0:1, cols]
            x = p_ref[:, cols].astype(F32) * scale_v[i, 0:1, cols] - mean
            pc[64 * i : 64 * i + 64, cols] = (x * gate).astype(BF16)
            both = jnp.concatenate([x, u_ref[:, cols].astype(F32) * gate], 0).astype(BF16)
            xws[i % 2][:, cols] = both
            return acc + both.astype(F32)

        acc = lax.fori_loop(0, 24, fill, jnp.zeros((128, 128), F32), unroll=24)
        return jnp.sum(acc, axis=1, keepdims=True)

    def large(i, first=0, last=F):
        nz[256 * i : 256 * i + 256, first:last] = dot_nt(zps[i][...], weight_v[first:last, :])

    def small_products(i, sums):
        tokens = slice(256 * i, 256 * i + 256)
        mean_row = jnp.transpose(meanb[tokens, :])[:1, :]
        vbt[i] = dot_nt(xws[i % 2][...], stored_v[i]) - sums * mean_row

    def gelu(i):
        @pl.loop(0, 16, unroll=16)
        def _(r):
            rows = pl.ds(r * 16, 16)
            here = pl.ds(i * 256 + r * 16, 16)
            for s in range(3):
                cols = slice(512 * s, 512 * s + 512)
                m = pre_v[i, rows, cols].astype(F32)
                h = 0.5 + 0.5 * jnp.tanh(m * (GELU_A + (GELU_A * 0.044715) * (m * m)))
                hid[here, cols] = (m * h).astype(BF16)

    def slopes(i):
        @pl.loop(0, 16, unroll=16)
        def _(r):
            rows = pl.ds(r * 16, 16)
            here = pl.ds(i * 256 + r * 16, 16)
            for s in range(3):
                cols = slice(512 * s, 512 * s + 512)
                m = pre_v[i, rows, cols].astype(F32)
                sq = m * m
                h = 0.5 + 0.5 * jnp.tanh(m * (GELU_A + (GELU_A * 0.044715) * sq))
                slope[here, cols] = h + (2.0 * m) * h * (1.0 - h) * (
                    GELU_A + (GELU_A * 0.134145) * sq
                )

    stored_copy(0).wait()
    sums = prep(0)
    stats(0)
    start_b()

    def copy_l(t, slot):
        return pltpu.make_async_remote_copy(
            src_ref=low_part.at[t],
            dst_ref=recv_l.at[slot],
            send_sem=send_l.at[0],
            recv_sem=got_l.at[0],
            device_id=(w, t),
            device_id_type=MESH,
        )

    @pl.loop(0, 6)
    def _(j):
        weight_copy(j).wait()

    stored_copy(1).wait()
    for i in range(4):
        pre_copy(i).wait()
    large(0)
    small_products(0, sums)
    stats(1)
    sums = prep(1)
    for i in range(4):
        gelu(i)
    for i in range(4):
        lt = dot_nt(at_ref[...], hid[256 * i : 256 * i + 256, :])
        low_part[2 * i] = lt[:, :128]
        low_part[2 * i + 1] = lt[:, 128:]

    @pl.loop(1, 8)
    def _(k):
        copy_l(lax.rem(n + k, 8), n).start()

    stored_copy(2).wait()
    large(1)
    small_products(1, sums)
    stats(2)
    sums = prep(2)

    def copy_c(dn, slot):
        return pltpu.make_async_remote_copy(
            src_ref=red,
            dst_ref=recv_c.at[slot],
            send_sem=send_c.at[0],
            recv_sem=got_c.at[0],
            device_id=(c_wide, dn),
            device_id_type=MESH,
        )

    my_c_slot = 2 * img + lax.rem(n, 2)
    recv_b[me_b] = own[me_b]
    all_of(recv_b, 15, send_b, got_b).wait_recv()
    red[...] = sum_of(recv_b, 16)

    @pl.loop(1, 9)
    def _(k):
        dn = lax.rem(n + k, 8)

        @pl.when(jnp.logical_or(k < 8, jnp.logical_not(c_self)))
        def _():
            copy_c(dn, my_c_slot).start()

    @pl.when(c_self)
    def _():
        recv_c[my_c_slot] = red[...]

    def copy_m(t, slot):
        return pltpu.make_async_remote_copy(
            src_ref=red_l,
            dst_ref=recv_m.at[slot],
            send_sem=send_m.at[0],
            recv_sem=got_m.at[0],
            device_id=(w, t),
            device_id_type=MESH,
        )

    recv_l[n] = low_part[n]
    all_of(recv_l, 7, send_l, got_l).wait_recv()
    red_l[...] = sum_of(recv_l, 8)
    recv_m[n] = red_l[...]

    @pl.loop(1, 8)
    def _(k):
        copy_m(lax.rem(n + k, 8), n).start()

    stored_copy(3).wait()
    large(2)
    small_products(2, sums)
    stats(3)
    sums = prep(3)
    slopes(0)
    slopes(1)
    small_products(3, sums)
    large(3, 0, F // 2)
    put = dot_nt(u_ref[...], pc[...])

    @pl.when(c_self)
    def _():
        all_of(recv_c, 7, send_c, got_c).wait_recv()

    @pl.when(jnp.logical_not(c_self))
    def _():
        all_of(recv_c, 8, send_c, got_c).wait_recv()

    all_of(recv_m, 7, send_m, got_m).wait_recv()

    t1 = []
    for i in range(4):
        tok = slice(256 * i, 256 * i + 256)
        lat = jnp.concatenate([recv_c[2 * i], recv_c[2 * i + 1]], 1)
        pat = (lat * VAE_INVERSE).astype(BF16)
        pf = pat.astype(F32)
        inv = jnp.transpose(invb[tok, :])[:1, :]
        vb = vbt[i]
        k_row = inv * inv * (jnp.sum(pf * vb[:64], axis=0, keepdims=True) * (1.0 / D))
        pu = put[:, 64 * i : 64 * i + 64]
        pu_hi = pu.astype(BF16)
        pu_lo = (pu - pu_hi.astype(F32)).astype(BF16)
        back = (inv * (dot_nn(pu_hi, pat) + dot_nn(pu_lo, pat) - k_row * vb[64:])).astype(BF16)
        ip = inv * pf
        ip_hi = ip.astype(BF16)
        ip_lo = (ip - ip_hi.astype(F32)).astype(BF16)
        backt[:, tok] = back
        stack = jnp.concatenate([ip_hi, ip_lo, ip_hi, back], 0)
        ltile[tok, :] = jnp.transpose(stack.astype(F32)).astype(BF16)
        ik = inv * k_row
        ikcol[tok, :] = jnp.transpose(jnp.broadcast_to(ik, (128, 256)))
        low = (jnp.concatenate([recv_m[2 * i], recv_m[2 * i + 1]], 1) * NORM).astype(BF16)
        klt[:, tok] = (-ik * low.astype(F32)).astype(BF16)
        t1.append(dot_nt(low, ip_hi) + dot_nt(low, ip_lo))
    klt[:, 1024:1280] = jnp.concatenate(t1, 1).astype(BF16)

    mine = pl.ds(pl.multiple_of(n * 384, 128), 384)
    up_t = dot_nn(klt[:, 1024:1280], pc[:, mine])
    for i in range(4):
        up_t += dot_nn(klt[:, 256 * i : 256 * i + 256], zps[i][:, mine])
    ubuf[0] = up_t[:, :256]
    ubuf[1] = pltpu.roll(up_t[:, 128:384], 192, 1)

    def copy_u(t, slot):
        return pltpu.make_async_remote_copy(
            src_ref=ubuf.at[lax.div(t, 8), pl.ds(pl.multiple_of(lax.rem(t, 8) * 8, 8), 8)],
            dst_ref=recv_u.at[slot],
            send_sem=send_u.at[0],
            recv_sem=got_u.at[0],
            device_id=(t, n),
            device_id_type=MESH,
        )

    @pl.loop(1, 16)
    def _(k):
        copy_u(lax.rem(w + k, 16), w).start()

    down_t = dot_nn(backt[...], hid[...]) * NORM
    for t in range(16):
        first = 96 * t // 128 * 128
        off = 96 * t - first
        if off + 96 <= 128:
            piece = down_t[:, first : first + 128]
            piece = pltpu.roll(piece, 128 - off, 1) if off else piece
        else:
            piece = pltpu.roll(down_t[:, first : first + 256], 256 - off, 1)[:, :128]
        dbuf[t] = piece

    def copy_d(t, slot):
        return pltpu.make_async_remote_copy(
            src_ref=dbuf.at[t],
            dst_ref=recv_d.at[slot],
            send_sem=send_d.at[0],
            recv_sem=got_d.at[0],
            device_id=(t, n),
            device_id_type=MESH,
        )

    @pl.loop(1, 16)
    def _(k):
        copy_d(lax.rem(w + k, 16), w).start()

    large(3, F // 2, F)
    slopes(2)
    slopes(3)

    def copy_e(dn, slot):
        return pltpu.make_async_remote_copy(
            src_ref=red_u,
            dst_ref=recv_e.at[slot],
            send_sem=send_e.at[0],
            recv_sem=got_e.at[0],
            device_id=(e_wide, dn),
            device_id_type=MESH,
        )

    my_e_slot = lax.rem(w, 8)
    recv_u[w] = ubuf[lax.div(w, 8), pl.ds(pl.multiple_of(my_e_slot * 8, 8), 8)]
    all_of(recv_u, 15, send_u, got_u).wait_recv()
    red_u[...] = sum_of(recv_u, 16)

    @pl.loop(1, 9)
    def _(k):
        dn = lax.rem(n + k, 8)

        @pl.when(jnp.logical_or(k < 8, jnp.logical_not(e_self)))
        def _():
            copy_e(dn, my_e_slot).start()

    @pl.when(e_self)
    def _():
        recv_e[my_e_slot] = red_u[...]

    nz[1024:1280, :] = dot_nt(pc[...], weight_v[...])

    def grads(i, h):
        cols = slice(768 * h, 768 * h + 768)
        q = nz[1024 + 64 * i : 1088 + 64 * i, cols]
        q_hi = q.astype(BF16)
        q_lo = (q - q_hi.astype(F32)).astype(BF16)
        right = jnp.concatenate([q_hi, q_hi, q_lo, at_ref[:, cols]], 0)
        prods[h][...] = dot_nn(ltile[256 * i : 256 * i + 256, :], right)

    def finish(i, h):
        @pl.loop(0, 16, unroll=16)
        def _(r):
            rows = pl.ds(r * 16, 16)
            here = pl.ds(i * 256 + r * 16, 16)
            coef = ikcol[here, :]
            coef = jnp.concatenate([coef] * 3, 1)
            for s in range(2):
                cols = slice(768 * h + 384 * s, 768 * h + 384 * s + 384)
                grad = prods[h][rows, 384 * s : 384 * s + 384] - coef * nz[here, cols]
                pre_v[i, rows, cols] = (grad * slope[here, cols]).astype(BF16)

    grads(0, 0)
    for i in range(4):
        grads(i, 1)
        finish(i, 0)
        if i < 3:
            grads(i + 1, 0)
        finish(i, 1)
        out_copy(i).start()

    recv_d[w] = dbuf[w]
    all_of(recv_d, 15, send_d, got_d).wait_recv()
    down_out[...] = sum_of(recv_d, 16)[:, :96]

    @pl.when(e_self)
    def _():
        all_of(recv_e, 7, send_e, got_e).wait_recv()

    @pl.when(jnp.logical_not(e_self))
    def _():
        all_of(recv_e, 8, send_e, got_e).wait_recv()

    up = jnp.concatenate([recv_e[k] for k in range(8)], 0)
    up_out[...] = up[:, :192]

    all_of(recv_b, 15, send_b, got_b).wait_send()
    all_of(recv_l, 7, send_l, got_l).wait_send()
    all_of(recv_m, 7, send_m, got_m).wait_send()
    all_of(recv_u, 15, send_u, got_u).wait_send()
    all_of(recv_d, 15, send_d, got_d).wait_send()

    @pl.when(c_self)
    def _():
        all_of(recv_c, 7, send_c, got_c).wait_send()

    @pl.when(jnp.logical_not(c_self))
    def _():
        all_of(recv_c, 8, send_c, got_c).wait_send()

    @pl.when(e_self)
    def _():
        all_of(recv_e, 7, send_e, got_e).wait_send()

    @pl.when(jnp.logical_not(e_self))
    def _():
        all_of(recv_e, 8, send_e, got_e).wait_send()

    @pl.loop(0, 4)
    def _(i):
        out_copy(i).wait()


def main(*args):
    dma = pltpu.SemaphoreType.DMA
    v = pltpu.VMEM
    anywhere = pl.BlockSpec(memory_space=pl.ANY)
    vmem = pl.BlockSpec(memory_space=pltpu.VMEM)
    return pl.pallas_call(
        main_kernel,
        out_shape=(
            jax.ShapeDtypeStruct((4, 256, F), BF16),
            jax.ShapeDtypeStruct((64, 192), F32),
            jax.ShapeDtypeStruct((64, 96), F32),
        ),
        in_specs=[anywhere] * 10,
        out_specs=(anywhere, vmem, vmem),
        scratch_shapes=[
            v((16, 64, 128), F32),
            v((16, 64, 128), F32),
            v((16, 64, 128), F32),
            v((64, 128), F32),
            v((8, 64, 128), F32),
            v((8, 64, 128), F32),
            v((8, 64, 128), F32),
            v((64, 128), F32),
            v((8, 64, 128), F32),
            v((2, 64, 256), F32),
            v((16, 8, 256), F32),
            v((8, 256), F32),
            v((8, 8, 256), F32),
            v((16, 64, 128), F32),
            v((16, 64, 128), F32),
            v((4, 256, D), BF16),
            v((4, 256, F), BF16),
            v((F, D), BF16),
            v((256, D), BF16),
            v((256, D), BF16),
            v((256, D), BF16),
            v((256, D), BF16),
            v((256, D), BF16),
            v((128, D), BF16),
            v((128, D), BF16),
            v((1024, F), BF16),
            v((1024, F), F32),
            v((1280, F), F32),
            v((256, F // 2), F32),
            v((256, F // 2), F32),
            v((16, 128, 128), BF16),
            v((144, 512), BF16),
            v((4, 130, 16, 128), BF16),
            v((64, D), BF16),
            v((64, D), BF16),
            v((4, D), BF16),
            v((4, D), BF16),
            v((1024, 128), F32),
            v((1024, 128), F32),
            v((4, 128, 256), F32),
            v((1024, 128), F32),
            v((1024, 256), BF16),
            v((64, 1024), BF16),
            v((64, 1280), BF16),
            v((64, F), BF16),
            v((4, 8, D), F32),
            v((4, 8, D), F32),
            dma((7,)),
            dma((4,)),
            dma((4,)),
            dma((6,)),
            dma((4,)),
            dma((1,)),
            dma((1,)),
            dma((1,)),
            dma((1,)),
            dma((1,)),
            dma((1,)),
            dma((1,)),
            dma((1,)),
            dma((1,)),
            dma((1,)),
            dma((1,)),
            dma((1,)),
            dma((1,)),
            dma((1,)),
            dma((1,)),
            dma((1,)),
        ],
        compiler_params=pltpu.CompilerParams(
            collective_id=0, has_side_effects=True, vmem_limit_bytes=62 * MIB
        ),
        name="main",
    )(*args)


def place_kernel(pre, up, down, pre_out, up_out, down_out, pre_v, up_v, down_v, sem_in, sem_out):
    pieces = [
        (pre.at[i, rows], pre_v.at[i, rows], pre_out.at[i, rows])
        for i in range(4)
        for rows in (pl.ds(0, 128), pl.ds(128, 128))
    ]
    pieces += [(up, up_v, up_out), (down, down_v, down_out)]
    into = [
        pltpu.make_async_copy(src, mid, sem_in.at[k]) for k, (src, mid, _) in enumerate(pieces)
    ]
    out = [
        pltpu.make_async_copy(mid, dst, sem_out.at[k]) for k, (_, mid, dst) in enumerate(pieces)
    ]
    for copy in into:
        copy.start()
    for first, second in zip(into, out):
        first.wait()
        second.start()
    for copy in out:
        copy.wait()


def place(*arrays):
    shapes = [(a.shape, a.dtype) for a in arrays]
    anywhere = pl.BlockSpec(memory_space=pl.ANY)
    return pl.pallas_call(
        place_kernel,
        out_shape=tuple(jax.ShapeDtypeStruct(*s) for s in shapes),
        in_specs=[anywhere] * 3,
        out_specs=(anywhere,) * 3,
        scratch_shapes=[pltpu.VMEM(*s) for s in shapes]
        + [pltpu.SemaphoreType.DMA((10,)), pltpu.SemaphoreType.DMA((10,))],
        compiler_params=pltpu.CompilerParams(vmem_limit_bytes=62 * MIB),
        name="place",
    )(*arrays)


def local(
    cotangent,
    decoder_kernel,
    patch_projection_rows,
    stored_hidden_state,
    output_norm_scale,
    output_gate,
    preactivation_input,
    frozen_down_weight,
    adapter_down_rows,
    adapter_up_rows,
):
    parts = main(
        cotangent[0],
        decoder_kernel.transpose(1, 2, 0).reshape(144, 512),
        stored_hidden_state,
        preactivation_input,
        frozen_down_weight,
        adapter_down_rows.T,
        adapter_up_rows,
        patch_projection_rows,
        output_norm_scale,
        output_gate,
    )
    pre_grad, up_grad, down_grad = place(*parts)
    return pre_grad, up_grad.T, down_grad.T


def solution(mesh):
    placed = (
        P("wide", "narrow", None, None),
        P(),
        P(),
        P(None, "wide", None),
        P(),
        P(),
        P(None, "wide", "narrow"),
        P("narrow", None),
        P("narrow", None),
        P(),
    )
    return jax.shard_map(
        local,
        mesh=mesh,
        in_specs=placed,
        out_specs=(P(None, "wide", "narrow"), P("wide", None), P(("narrow", "wide"), None)),
        check_vma=False,
    )
```
